128 devices in a mesh: cfg: 2 (over x_lo), blk: 8 (over z, core), uly: 8 (over x_hi, y).
Axes of the slice: x: 4 (x_hi: 2, x_lo: 2; x = x_hi * 2 + x_lo), y: 4, z: 4, core: 2. Of those that a mesh axis runs over, the one named last changes fastest.
Arguments:
- new_queries: bfloat16 [8192, 6144], P(('cfg', 'blk', 'uly')), parts along dimension 0, may hold values from -15 to 15
- new_keys: bfloat16 [8192, 6144], P(('cfg', 'blk', 'uly')), parts along dimension 0, may hold values from -6 to 6
- new_values: bfloat16 [8192, 6144], P(('cfg', 'blk', 'uly')), parts along dimension 0, may hold values from -6 to 6
- context_keys: bfloat16 [16384, 6144], P(('cfg', 'blk'), 'uly'), parts along dimension 0, may hold values from -6 to 6
- context_values: bfloat16 [16384, 6144], P(('cfg', 'blk'), 'uly'), parts along dimension 0, may hold values from -6 to 6
- keep_flags: int32 [32, 96], replicated, may hold values from 0 to 1, as said below
Outputs:
- attended: bfloat16 [8192, 6144], P(('cfg', 'blk', 'uly')), parts along dimension 0
The draws below stay inside these ranges and needn't reach their ends.
There are 2 independent parts, one for each index of `cfg`. The reference program is written for one: setup_inputs(seed, part) draws one part's arguments, and reference() takes and returns one part's arrays. A program takes and returns all parts, laid end to end along the dimension named above; an argument that names none is the same for every part. Nothing has to cross between parts.
Inputs may be any that keep to these rules, and one draw needn't show every extreme that they name: keep_flags[i, 0] and keep_flags[i, 64 + i] are 1 for every query block i; at least one query block keeps every key block.
All inputs are finite; a program needn't handle non-finite values.
Results may differ from the reference program's by a relative error of at most 0.017.
Values may be sent and summed in bfloat16 or wider, within the bound.
A program may use at most 128 MiB of HBM per device.

```python
import jax
import jax.numpy as jnp
from jax import lax

H = 48
DH = 128
D = 6144
TILE = 128
CH = 4096
CTX = 8192
QT = 32
KT = 96


def draw_new_queries(key, part):
    key = jax.random.fold_in(key, 11)
    base = jnp.clip(2.5 * jax.random.normal(key, (CH, D), jnp.float32), -15.0, 15.0)
    return base.astype(jnp.bfloat16)


def draw_context_keys(key, part):
    key = jax.random.fold_in(key, 12)
    base = jnp.clip(jax.random.normal(key, (CTX, D), jnp.float32), -6.0, 6.0)
    return base.astype(jnp.bfloat16)


def draw_keep_flags(key, part):
    key = jax.random.fold_in(key, 13)
    roll_key, pick_key, extra_key = jax.random.split(key, 3)
    query_tile = jnp.arange(QT)[:, None]
    key_tile = jnp.arange(KT)[None, :]
    distance = jnp.abs(CTX // TILE + query_tile - key_tile)
    threshold = 4096 // (4 + distance)
    rolled = jax.random.randint(roll_key, (QT, KT), 0, 1024)
    chosen = jax.random.randint(pick_key, (), 0, QT)
    extra = jax.random.randint(extra_key, (QT,), 0, 16) == 0
    global_rows = (jnp.arange(QT) == chosen) | extra
    kept = (rolled < threshold) | (key_tile == 0) | (distance == 0) | global_rows[:, None]
    return kept.astype(jnp.int32)


def block_levels(key, extent, pieces, low, largest):
    def one(position, shards_of):
        steps = jax.random.uniform(jax.random.fold_in(jax.random.fold_in(key, 6), position), (shards_of,), jnp.float32, low / len(pieces), largest / len(pieces))
        return jnp.repeat(jnp.exp(steps), extent[position] // shards_of).reshape((-1,) + (1,) * (len(extent) - position - 1))

    loudness = one(*pieces[0])
    for cut in pieces[1:]:
        loudness = loudness * one(*cut)
    return loudness


def noise(rng, extent, scale, limit, shards=(), kind=jnp.bfloat16):
    gain = block_levels(rng, extent, shards, -0.22, 0.18) if shards else 1.0
    array = jax.random.normal(rng, extent, jnp.float32) * scale * gain
    return jnp.minimum(jnp.maximum(array, -limit), limit).astype(kind)


def setup_inputs(seed: int = 0, part: int = 0) -> dict:
    streams_of = jax.random.split(jax.random.key(seed), 7)
    part_keys = jax.random.split(jax.random.fold_in(streams_of[6], part), 7)
    new_queries = draw_new_queries(jax.random.fold_in(jax.random.fold_in(streams_of[6], part), 71), part)
    new_keys = noise(part_keys[1], (CH, D), 1.0, 6.0, ((0, 64),))
    new_values = noise(part_keys[2], (CH, D), 1.0, 6.0, ((0, 64),))
    context_keys = draw_context_keys(jax.random.fold_in(jax.random.fold_in(streams_of[6], part), 71), part)
    context_values = noise(part_keys[4], (CTX, D), 1.0, 6.0, ((0, 8), (1, 8)))
    keep_flags = draw_keep_flags(jax.random.fold_in(streams_of[6], 71), part)
    return dict(new_queries=new_queries, new_keys=new_keys, new_values=new_values, context_keys=context_keys, context_values=context_values, keep_flags=keep_flags)


def reference(new_queries, new_keys, new_values, context_keys, context_values, keep_flags):
    all_keys = jnp.concatenate([context_keys, new_keys], axis=0)
    all_values = jnp.concatenate([context_values, new_values], axis=0)
    query_count = new_queries.shape[0]
    key_count = all_keys.shape[0]
    allowed = jnp.repeat(jnp.repeat(keep_flags > 0, TILE, axis=0), TILE, axis=1)
    query_heads = new_queries.reshape(query_count, H, DH).transpose(1, 0, 2)
    key_heads = all_keys.reshape(key_count, H, DH).transpose(1, 0, 2)
    value_heads = all_values.reshape(key_count, H, DH).transpose(1, 0, 2)

    def one_head(head_items):
        scores = jnp.dot(head_items[0], head_items[1].T, preferred_element_type=jnp.float32) * (DH ** -0.5)
        scores = jnp.where(allowed, scores, -1.0e30)
        row_max = jnp.max(scores, axis=1, keepdims=True)
        probs = jnp.where(allowed, jnp.exp(scores - row_max), 0.0)
        denom = jnp.sum(probs, axis=1, keepdims=True)
        summed = jnp.dot(probs.astype(jnp.bfloat16), head_items[2], preferred_element_type=jnp.float32)
        return (summed / denom).astype(jnp.bfloat16)

    outputs = lax.map(one_head, (query_heads, key_heads, value_heads))
    return outputs.transpose(1, 0, 2).reshape(query_count, H * DH)
```

```python
import functools

import jax
import jax.numpy as jnp
from jax import lax
from jax.experimental import pallas as pl
from jax.experimental.pallas import tpu as pltpu
from jax.sharding import PartitionSpec as P

DH = 128
TILE = 128
HEADS = 6
ROWS = 144
LOW = -1e30
LOG2 = 1.4426950408889634 * DH ** (-0.5)


def attend_kernel(order_ref, count_ref, q_ref, k_ref, v_ref, o_ref, lse_ref, vt, acc, top):
    step = pl.program_id(0)
    tiles = vt.shape[0]

    @pl.when(step == 0)
    def _():
        def turn(t, carry):
            rows = pl.ds(pl.multiple_of(t * TILE, TILE), TILE)
            for h in range(HEADS):
                vt[t, h * ROWS : h * ROWS + DH, :] = v_ref[rows, h * DH : (h + 1) * DH].T
                vt[t, h * ROWS + DH : (h + 1) * ROWS, :] = jnp.ones((ROWS - DH, TILE), jnp.bfloat16)
            return carry

        lax.fori_loop(0, tiles, turn, 0)

    acc[...] = jnp.zeros_like(acc)
    top[...] = jnp.full_like(top, LOW)
    count = count_ref[step]

    def visit(picked):
        for h in range(HEADS):
            cols = slice(h * DH, (h + 1) * DH)
            q = q_ref[:, cols]
            s = [
                lax.dot_general(
                    k_ref[pl.ds(pl.multiple_of(t * TILE, TILE), TILE), cols],
                    q,
                    (((1,), (1,)), ((), ())),
                    preferred_element_type=jnp.float32,
                )
                for t in picked
            ]
            s = s[0] if len(s) == 1 else jnp.concatenate(s, axis=0)
            old = top[h : h + 1, :]
            new = jnp.maximum(old, jnp.max(s, axis=0, keepdims=True))
            top[h : h + 1, :] = new
            p = jnp.exp2((s - new) * LOG2).astype(jnp.bfloat16)
            scale = jnp.exp2((old - new) * LOG2)
            vs = [vt[t, h * ROWS : (h + 1) * ROWS, :] for t in picked]
            vs = vs[0] if len(vs) == 1 else jnp.concatenate(vs, axis=1)
            acc[h] = acc[h] * scale + jnp.dot(vs, p, preferred_element_type=jnp.float32)

    def pair(j, carry):
        visit([order_ref[step, 2 * j], order_ref[step, 2 * j + 1]])
        return carry

    lax.fori_loop(0, count // 2, pair, 0)

    @pl.when(count % 2 == 1)
    def _():
        visit([order_ref[step, count - 1]])

    for h in range(HEADS):
        total = acc[h, DH : DH + 1, :]
        any_key = total > 0
        safe = jnp.where(any_key, total, 1.0)
        o_ref[0, h * DH : (h + 1) * DH, :] = (acc[h, :DH, :] * (1.0 / safe)).astype(jnp.bfloat16)
        lse_ref[0, h : h + 1, :] = jnp.where(any_key, top[h : h + 1, :] * LOG2 + jnp.log2(safe), LOW)
    lse_ref[0, HEADS:, :] = jnp.full((8 - HEADS, TILE), LOW, jnp.float32)


def attend(order, counts, queries, keys, values):
    steps = queries.shape[0] // TILE
    tiles = keys.shape[0] // TILE
    width = queries.shape[1]
    whole = pl.BlockSpec(keys.shape, lambda i, *_: (0, 0))
    return pl.pallas_call(
        attend_kernel,
        out_shape=(
            jax.ShapeDtypeStruct((steps, width, TILE), jnp.bfloat16),
            jax.ShapeDtypeStruct((steps, 8, TILE), jnp.float32),
        ),
        grid_spec=pltpu.PrefetchScalarGridSpec(
            num_scalar_prefetch=2,
            grid=(steps,),
            in_specs=[pl.BlockSpec((TILE, width), lambda i, *_: (i, 0)), whole, whole],
            out_specs=(
                pl.BlockSpec((1, width, TILE), lambda i, *_: (i, 0, 0)),
                pl.BlockSpec((1, 8, TILE), lambda i, *_: (i, 0, 0)),
            ),
            scratch_shapes=[
                pltpu.VMEM((tiles, HEADS * ROWS, TILE), jnp.bfloat16),
                pltpu.VMEM((HEADS, ROWS, TILE), jnp.float32),
                pltpu.VMEM((8, TILE), jnp.float32),
            ],
        ),
        compiler_params=pltpu.CompilerParams(vmem_limit_bytes=40 * 1024 * 1024),
        cost_estimate=pl.CostEstimate(flops=6 * 10**9, bytes_accessed=18 * 10**6, transcendentals=12 * 10**6),
    )(order, counts, queries, keys, values)


def kept_tiles(keep_flags, ctx_tiles, span_tiles, blk, cycle):
    ctx = lax.dynamic_slice_in_dim(keep_flags, blk * ctx_tiles, ctx_tiles, 1)
    span = lax.dynamic_slice_in_dim(keep_flags, cycle * ctx_tiles + blk * span_tiles, span_tiles, 1)
    mine = (jnp.concatenate([ctx, span], axis=1) > 0).astype(jnp.int32)
    n = mine.shape[1]
    place = jnp.cumsum(mine, axis=1) - 1
    slot = jnp.arange(n, dtype=jnp.int32)
    hit = (place[:, :, None] == slot[None, None, :]) & (mine[:, :, None] > 0)
    order = jnp.sum(jnp.where(hit, slot[None, :, None], 0), axis=1)
    return order, jnp.sum(mine, axis=1)


def shards(new_queries, new_keys, new_values, context_keys, context_values, keep_flags):
    span_queries = lax.all_to_all(new_queries, "uly", split_axis=1, concat_axis=0, tiled=True)
    queries = lax.all_gather(span_queries, "blk", axis=0, tiled=True)
    span_keys = lax.all_to_all(new_keys, "uly", split_axis=1, concat_axis=0, tiled=True)
    span_values = lax.all_to_all(new_values, "uly", split_axis=1, concat_axis=0, tiled=True)
    keys = jnp.concatenate([context_keys, span_keys], axis=0)
    values = jnp.concatenate([context_values, span_values], axis=0)
    cycle = lax.axis_size("blk")
    blk = lax.axis_index("blk")
    order, counts = kept_tiles(
        keep_flags, context_keys.shape[0] // TILE, span_keys.shape[0] // TILE, blk, cycle
    )
    part, lse = attend(order, counts, queries, keys, values)
    lse = lse[:, :HEADS, :]
    best = lax.pmax(lse, "blk")
    weight = jnp.exp2(lse - best)
    steps = part.shape[0]
    scaled = part.reshape(steps, HEADS, DH, TILE).astype(jnp.float32) * weight[:, :, None, :]
    weighted = lax.psum_scatter(scaled, "blk", scatter_dimension=0, tiled=True)
    totals = lax.psum_scatter(weight, "blk", scatter_dimension=0, tiled=True)
    mine = (weighted / totals[:, :, None, :]).astype(jnp.bfloat16)
    attended = mine.transpose(0, 3, 1, 2).reshape(-1, HEADS * DH)
    return lax.all_to_all(attended, "uly", split_axis=0, concat_axis=1, tiled=True)


def solution(mesh):
    in_specs = (
        P(("cfg", "blk", "uly"), None),
        P(("cfg", "blk", "uly"), None),
        P(("cfg", "blk", "uly"), None),
        P(("cfg", "blk"), "uly"),
        P(("cfg", "blk"), "uly"),
        P(),
    )
    out_specs = P(("cfg", "blk", "uly"), None)
    return jax.shard_map(shards, mesh=mesh, in_specs=in_specs, out_specs=out_specs, check_vma=False)
```

```python
import functools

import jax
import jax.numpy as jnp
from jax import lax
from jax.experimental import pallas as pl
from jax.experimental.pallas import tpu as pltpu
from jax.sharding import PartitionSpec as P

DH = 128
TILE = 128
HEADS = 6
WIDTH = HEADS * DH
ROWS = 144
PIECE = WIDTH + 16
GROUP = 4
PER = 4
LOW = -1e30
LOG2 = 1.4426950408889634 * DH ** (-0.5)
MESH = pl.DeviceIdType.MESH


def split_low(x):
    high = x.astype(jnp.bfloat16).astype(jnp.float32)
    return jnp.concatenate([high, x - high], axis=0).astype(jnp.bfloat16)


def attend_kernel(order_ref, count_ref, q_ref, k_ref, v_ref, o_ref, vt, acc, top):
    step = pl.program_id(0)
    tiles = vt.shape[0]

    @pl.when(step == 0)
    def _():
        def turn(t, carry):
            rows = pl.ds(pl.multiple_of(t * TILE, TILE), TILE)
            for h in range(HEADS):
                vt[t, h * ROWS : h * ROWS + DH, :] = v_ref[rows, h * DH : (h + 1) * DH].T
                vt[t, h * ROWS + DH : (h + 1) * ROWS, :] = jnp.ones((ROWS - DH, TILE), jnp.bfloat16)
            return carry

        lax.fori_loop(0, tiles, turn, 0)
        top[...] = jnp.full_like(top, LOW)

    def one(sub, carry):
        tile = step * PER + sub
        q_rows = pl.ds(pl.multiple_of(sub * TILE, TILE), TILE)
        count = count_ref[tile]

        def scores(h, picked):
            cols = slice(h * DH, (h + 1) * DH)
            ks = [k_ref[pl.ds(pl.multiple_of(t * TILE, TILE), TILE), cols] for t in picked]
            return lax.dot_general(
                jnp.concatenate(ks, axis=0),
                q_ref[q_rows, cols],
                (((1,), (1,)), ((), ())),
                preferred_element_type=jnp.float32,
            )

        def weigh(h, picked, s, first):
            new = jnp.max(s, axis=0, keepdims=True)
            if not first:
                old = top[h : h + 1, :]
                new = jnp.maximum(old, new)
                scale = jnp.exp2((old - new) * LOG2)
            top[h : h + 1, :] = new
            p = jnp.exp2((s - new) * LOG2).astype(jnp.bfloat16)
            vs = jnp.concatenate([vt[t, h * ROWS : (h + 1) * ROWS, :] for t in picked], axis=1)
            got = jnp.dot(vs, p, preferred_element_type=jnp.float32)
            acc[h] = got if first else acc[h] * scale + got

        def visit(picked, first):
            all_scores = [scores(h, picked) for h in range(HEADS)]
            for h in range(HEADS):
                weigh(h, picked, all_scores[h], first)

        def none():
            acc[...] = jnp.zeros_like(acc)

        def lead_visit(n):
            visit([order_ref[tile, a] for a in range(n)], True)

        lead = jnp.where(count == 0, 0, lax.rem(count + GROUP - 1, GROUP) + 1)
        lax.switch(lead, [none] + [functools.partial(lead_visit, n) for n in range(1, GROUP + 1)])

        def more(j, inner):
            visit([order_ref[tile, lead + GROUP * j + a] for a in range(GROUP)], False)
            return inner

        lax.fori_loop(0, (count - lead) // GROUP, more, 0)

        totals = [acc[h, DH : DH + 1, :] for h in range(HEADS)]
        for h in range(HEADS):
            safe = jnp.where(totals[h] > 0, totals[h], 1.0)
            o_ref[sub, h * DH : (h + 1) * DH, :] = (acc[h, :DH, :] * (1.0 / safe)).astype(jnp.bfloat16)
        total = jnp.concatenate(totals + [jnp.zeros((8 - HEADS, TILE), jnp.float32)], axis=0)
        found = total > 0
        lse = jnp.where(found, top[...] * LOG2 + jnp.log2(jnp.where(found, total, 1.0)), LOW)
        o_ref[sub, WIDTH:PIECE, :] = split_low(lse)
        return carry

    lax.fori_loop(0, PER, one, 0)


def attend(order, counts, queries, keys, values):
    steps = queries.shape[0] // TILE
    tiles = keys.shape[0] // TILE
    whole = pl.BlockSpec(keys.shape, lambda i, *_: (0, 0))
    return pl.pallas_call(
        attend_kernel,
        out_shape=jax.ShapeDtypeStruct((steps, PIECE, TILE), jnp.bfloat16),
        grid_spec=pltpu.PrefetchScalarGridSpec(
            num_scalar_prefetch=2,
            grid=(steps // PER,),
            in_specs=[pl.BlockSpec((TILE * PER, WIDTH), lambda i, *_: (i, 0)), whole, whole],
            out_specs=pl.BlockSpec((PER, PIECE, TILE), lambda i, *_: (i, 0, 0)),
            scratch_shapes=[
                pltpu.VMEM((tiles, HEADS * ROWS, TILE), jnp.bfloat16),
                pltpu.VMEM((HEADS, ROWS, TILE), jnp.float32),
                pltpu.VMEM((8, TILE), jnp.float32),
            ],
        ),
        compiler_params=pltpu.CompilerParams(vmem_limit_bytes=48 * 1024 * 1024),
        cost_estimate=pl.CostEstimate(flops=6 * 10**9, bytes_accessed=18 * 10**6, transcendentals=12 * 10**6),
    )(order, counts, queries, keys, values)


def merge(pieces):
    logs = []
    for ref, at in pieces:
        both = ref[at, WIDTH:PIECE, :].astype(jnp.float32)
        logs.append(both[:8] + both[8:])
    best = functools.reduce(jnp.maximum, logs)
    weights = [jnp.exp2(log - best) for log in logs]
    total = functools.reduce(jnp.add, weights)
    inverse = 1.0 / total
    shares = [w * inverse for w in weights]
    return shares, best + jnp.log2(total)


def head_sum(pieces, shares, h):
    found = None
    for (ref, at), share in zip(pieces, shares):
        term = ref[at, h * DH : (h + 1) * DH, :].astype(jnp.float32) * share[h : h + 1, :]
        found = term if found is None else found + term
    return found


def join_kernel(
    zs, part_ref, out_ref, own, sib, far, near, send_far, send_near, done,
    own_sem, sib_send, sib_recv, far_send, far_recv, near_send, near_recv, out_send, out_recv, out_local,
):
    blk = lax.axis_index("blk")
    uly = lax.axis_index("uly")
    z, core = blk // 2, blk % 2
    ring = [lax.rem(z + d, zs) for d in (2, 1, zs - 1, 0)]
    sibling = {"blk": z * 2 + 1 - core}
    ahead = {"blk": ring[1] * 2 + core}
    behind = {"blk": ring[2] * 2 + core}
    ulys = lax.axis_size("uly")
    tiles = own.shape[1]

    barrier = pltpu.get_barrier_semaphore()
    for device in (sibling, ahead, behind):
        pl.semaphore_signal(barrier, inc=1, device_id=device, device_id_type=MESH)
    for d in range(1, ulys):
        pl.semaphore_signal(barrier, inc=1, device_id={"uly": lax.rem(uly + d, ulys)}, device_id_type=MESH)

    def own_copy(slot, t):
        index = (ring[slot] * 2 + core) * tiles + t
        return pltpu.make_async_copy(part_ref.at[index], own.at[slot, t], own_sem.at[slot, t])

    def sib_copy(slot, t):
        index = (ring[slot] * 2 + 1 - core) * tiles + t
        return pltpu.make_async_remote_copy(
            src_ref=part_ref.at[index], dst_ref=sib.at[slot, t],
            send_sem=sib_send.at[slot, t], recv_sem=sib_recv.at[slot, t],
            device_id=sibling, device_id_type=MESH,
        )

    def far_copy(t):
        return pltpu.make_async_remote_copy(
            src_ref=send_far.at[t], dst_ref=far.at[t],
            send_sem=far_send.at[t], recv_sem=far_recv.at[t],
            device_id=ahead if t < 2 else behind, device_id_type=MESH,
        )

    def near_copy(way, t):
        return pltpu.make_async_remote_copy(
            src_ref=send_near.at[way, t], dst_ref=near.at[way, t],
            send_sem=near_send.at[way, t], recv_sem=near_recv.at[way, t],
            device_id=ahead if way == 0 else behind, device_id_type=MESH,
        )

    order = (
        [(0, 0), (0, 2), (0, 1), (0, 3), (1, 2), (2, 0), (1, 3), (2, 1), (1, 0), (2, 2), (1, 1), (2, 3)]
        + [(3, 0), (3, 2), (3, 1), (3, 3)]
    )
    for slot, t in order:
        own_copy(slot, t).start()
    pl.semaphore_wait(barrier, 3 + ulys - 1)
    for slot, t in order:
        sib_copy(slot, t).start()

    def ready(slot, t):
        own_copy(slot, t).wait()
        sib_copy(slot, t).wait_recv()
        return [(own.at[slot], t), (sib.at[slot], t)]

    def store(pieces, dst):
        shares, log = merge(pieces)
        for h in range(HEADS):
            dst[h * DH : (h + 1) * DH, :] = head_sum(pieces, shares, h).astype(jnp.bfloat16)
        dst[WIDTH:PIECE, :] = split_low(log)

    for t in (0, 2, 1, 3):
        store(ready(0, t), send_far.at[t])
        far_copy(t).start()
    for way, t in ((0, 2), (1, 0), (0, 3), (1, 1)):
        store(ready(way + 1, t), send_near.at[way, t])
        near_copy(way, t).start()
    for way, t in ((0, 0), (1, 2), (0, 1), (1, 3)):
        pieces = ready(way + 1, t)
        far_copy(t).wait_recv()
        store(pieces + [(far, t)], send_near.at[way, t])
        near_copy(way, t).start()

    half = out_ref.shape[0]

    def out_copy(u):
        return pltpu.make_async_remote_copy(
            src_ref=done.at[u], dst_ref=out_ref.at[:, pl.ds(pl.multiple_of(uly * WIDTH, WIDTH), WIDTH)],
            send_sem=out_send.at[u], recv_sem=out_recv.at[uly],
            device_id={"uly": u}, device_id_type=MESH,
        )

    def out_keep(u):
        return pltpu.make_async_copy(
            done.at[u], out_ref.at[:, pl.ds(pl.multiple_of(uly * WIDTH, WIDTH), WIDTH)], out_local
        )

    for t in (0, 2, 1, 3):
        pieces = ready(3, t)
        near_copy(0, t).wait_recv()
        near_copy(1, t).wait_recv()
        pieces = pieces + [(near.at[0], t), (near.at[1], t)]
        shares, log = merge(pieces)
        for h in range(HEADS):
            flat = head_sum(pieces, shares, h).astype(jnp.bfloat16).T
            for j in range(2):
                done[2 * t + j, :, h * DH : (h + 1) * DH] = flat[j * half : (j + 1) * half]
        for j in range(2):
            u = 2 * t + j

            @pl.when(uly != u)
            def _():
                out_copy(u).start()

            @pl.when(uly == u)
            def _():
                out_keep(u).start()

    out_keep(0).wait()
    for u in range(ulys):

        @pl.when(uly != u)
        def _():
            pltpu.make_async_remote_copy(
                src_ref=done.at[u], dst_ref=out_ref.at[:, u * WIDTH : (u + 1) * WIDTH],
                send_sem=out_send.at[u], recv_sem=out_recv.at[u],
                device_id={"uly": u}, device_id_type=MESH,
            ).wait()

    for slot, t in order:
        sib_copy(slot, t).wait_send()
    for t in range(tiles):
        far_copy(t).wait_send()
        near_copy(0, t).wait_send()
        near_copy(1, t).wait_send()


def join(part, rows, zs, ulys):
    tiles = part.shape[0] // (2 * zs)
    piece = (PIECE, TILE)
    dma = pltpu.SemaphoreType.DMA
    return pl.pallas_call(
        functools.partial(join_kernel, zs),
        out_shape=jax.ShapeDtypeStruct((rows, ulys * WIDTH), jnp.bfloat16),
        in_specs=[pl.BlockSpec(memory_space=pl.ANY)],
        out_specs=pl.BlockSpec(memory_space=pl.ANY),
        scratch_shapes=[
            pltpu.VMEM((4, tiles) + piece, jnp.bfloat16),
            pltpu.VMEM((4, tiles) + piece, jnp.bfloat16),
            pltpu.VMEM((tiles,) + piece, jnp.bfloat16),
            pltpu.VMEM((2, tiles) + piece, jnp.bfloat16),
            pltpu.VMEM((tiles,) + piece, jnp.bfloat16),
            pltpu.VMEM((2, tiles) + piece, jnp.bfloat16),
            pltpu.VMEM((ulys, rows, WIDTH), jnp.bfloat16),
            dma((4, tiles)), dma((4, tiles)), dma((4, tiles)),
            dma((tiles,)), dma((tiles,)),
            dma((2, tiles)), dma((2, tiles)),
            dma((ulys,)), dma((ulys,)), dma,
        ],
        compiler_params=pltpu.CompilerParams(
            collective_id=1, has_side_effects=True, vmem_limit_bytes=48 * 1024 * 1024
        ),
        cost_estimate=pl.CostEstimate(flops=2 * 10**7, bytes_accessed=10**7, transcendentals=10**5),
    )(part)


def kept_tiles(keep_flags, ctx_tiles, span_tiles, blk, cycle):
    ctx = lax.dynamic_slice_in_dim(keep_flags, blk * ctx_tiles, ctx_tiles, 1)
    span = lax.dynamic_slice_in_dim(keep_flags, cycle * ctx_tiles + blk * span_tiles, span_tiles, 1)
    mine = (jnp.concatenate([ctx, span], axis=1) > 0).astype(jnp.int32)
    n = mine.shape[1]
    place = jnp.cumsum(mine, axis=1) - 1
    slot = jnp.arange(n, dtype=jnp.int32)
    hit = (place[:, :, None] == slot[None, None, :]) & (mine[:, :, None] > 0)
    order = jnp.sum(jnp.where(hit, slot[None, :, None], 0), axis=1)
    return order, jnp.sum(mine, axis=1)


def shards(new_queries, new_keys, new_values, context_keys, context_values, keep_flags):
    span_queries = lax.all_to_all(new_queries, "uly", split_axis=1, concat_axis=0, tiled=True)
    queries = lax.all_gather(span_queries, "blk", axis=0, tiled=True)
    span_keys = lax.all_to_all(new_keys, "uly", split_axis=1, concat_axis=0, tiled=True)
    span_values = lax.all_to_all(new_values, "uly", split_axis=1, concat_axis=0, tiled=True)
    keys = jnp.concatenate([context_keys, span_keys], axis=0)
    values = jnp.concatenate([context_values, span_values], axis=0)
    cycle = lax.axis_size("blk")
    blk = lax.axis_index("blk")
    order, counts = kept_tiles(
        keep_flags, context_keys.shape[0] // TILE, span_keys.shape[0] // TILE, blk, cycle
    )
    part = attend(order, counts, queries, keys, values)
    return join(part, new_queries.shape[0], cycle // 2, lax.axis_size("uly"))


def solution(mesh):
    in_specs = (
        P(("cfg", "blk", "uly"), None),
        P(("cfg", "blk", "uly"), None),
        P(("cfg", "blk", "uly"), None),
        P(("cfg", "blk"), "uly"),
        P(("cfg", "blk"), "uly"),
        P(),
    )
    out_specs = P(("cfg", "blk", "uly"), None)
    return jax.shard_map(shards, mesh=mesh, in_specs=in_specs, out_specs=out_specs, check_vma=False)
```

```python
import functools

import jax
import jax.numpy as jnp
from jax import lax
from jax.experimental import pallas as pl
from jax.experimental.pallas import tpu as pltpu
from jax.sharding import PartitionSpec as P

DH = 128
TILE = 128
HEADS = 6
WIDTH = HEADS * DH
ROWS = 144
PIECE = WIDTH + 16
GROUP = 4
PER = 4
LOW = -1e30
LOG2 = 1.4426950408889634 * DH ** (-0.5)
MESH = pl.DeviceIdType.MESH


def split_low(x):
    high = x.astype(jnp.bfloat16).astype(jnp.float32)
    return jnp.concatenate([high, x - high], axis=0).astype(jnp.bfloat16)


def attend_kernel(
    blk_ref, flags_ref, q_ref, ck_ref, sk_ref, cv_ref, sv_ref, o_ref, k_ref, v_ref, vt, acc, top, order_ref, sems
):
    step = pl.program_id(0)
    tiles = vt.shape[0]
    ctx_rows = ck_ref.shape[0]
    ctx_tiles = ctx_rows // TILE
    span_tiles = tiles - ctx_tiles
    blk = blk_ref[0]
    first_span = flags_ref.shape[1] - flags_ref.shape[0]

    @pl.when(step == 0)
    def _():
        copies = [
            pltpu.make_async_copy(cv_ref, v_ref.at[:ctx_rows], sems.at[0]),
            pltpu.make_async_copy(sv_ref, v_ref.at[ctx_rows:], sems.at[1]),
            pltpu.make_async_copy(ck_ref, k_ref.at[:ctx_rows], sems.at[2]),
            pltpu.make_async_copy(sk_ref, k_ref.at[ctx_rows:], sems.at[3]),
        ]
        for copy in copies:
            copy.start()
        copies[0].wait()
        copies[1].wait()

        def turn(t, carry):
            rows = pl.ds(pl.multiple_of(t * TILE, TILE), TILE)
            for h in range(HEADS):
                vt[t, h * ROWS : h * ROWS + DH, :] = v_ref[rows, h * DH : (h + 1) * DH].T
                vt[t, h * ROWS + DH : (h + 1) * ROWS, :] = jnp.ones((ROWS - DH, TILE), jnp.bfloat16)
            return carry

        lax.fori_loop(0, tiles, turn, 0)
        top[...] = jnp.full_like(top, LOW)
        copies[2].wait()
        copies[3].wait()

    def one(sub, carry):
        tile = step * PER + sub
        q_rows = pl.ds(pl.multiple_of(sub * TILE, TILE), TILE)
        count = jnp.int32(0)
        for t in range(tiles):
            column = blk * ctx_tiles + t if t < ctx_tiles else first_span + blk * span_tiles + t - ctx_tiles
            order_ref[count] = t
            count = count + jnp.where(flags_ref[tile, column] > 0, 1, 0)

        def scores(h, picked):
            cols = slice(h * DH, (h + 1) * DH)
            ks = [k_ref[pl.ds(pl.multiple_of(t * TILE, TILE), TILE), cols] for t in picked]
            return lax.dot_general(
                jnp.concatenate(ks, axis=0),
                q_ref[q_rows, cols],
                (((1,), (1,)), ((), ())),
                preferred_element_type=jnp.float32,
            )

        def weigh(h, picked, s, first):
            new = jnp.max(s, axis=0, keepdims=True)
            if not first:
                old = top[h : h + 1, :]
                new = jnp.maximum(old, new)
                scale = jnp.exp2((old - new) * LOG2)
            top[h : h + 1, :] = new
            p = jnp.exp2((s - new) * LOG2).astype(jnp.bfloat16)
            vs = jnp.concatenate([vt[t, h * ROWS : (h + 1) * ROWS, :] for t in picked], axis=1)
            got = jnp.dot(vs, p, preferred_element_type=jnp.float32)
            acc[h] = got if first else acc[h] * scale + got

        def visit(picked, first):
            all_scores = [scores(h, picked) for h in range(HEADS)]
            for h in range(HEADS):
                weigh(h, picked, all_scores[h], first)

        def none():
            acc[...] = jnp.zeros_like(acc)

        def lead_visit(n):
            visit([order_ref[a] for a in range(n)], True)

        lead = jnp.where(count == 0, 0, lax.rem(count + GROUP - 1, GROUP) + 1)
        lax.switch(lead, [none] + [functools.partial(lead_visit, n) for n in range(1, GROUP + 1)])

        def more(j, inner):
            visit([order_ref[lead + GROUP * j + a] for a in range(GROUP)], False)
            return inner

        lax.fori_loop(0, (count - lead) // GROUP, more, 0)

        totals = [acc[h, DH : DH + 1, :] for h in range(HEADS)]
        for h in range(HEADS):
            safe = jnp.where(totals[h] > 0, totals[h], 1.0)
            o_ref[sub, h * DH : (h + 1) * DH, :] = (acc[h, :DH, :] * (1.0 / safe)).astype(jnp.bfloat16)
        total = jnp.concatenate(totals + [jnp.zeros((8 - HEADS, TILE), jnp.float32)], axis=0)
        found = total > 0
        lse = jnp.where(found, top[...] * LOG2 + jnp.log2(jnp.where(found, total, 1.0)), LOW)
        o_ref[sub, WIDTH:PIECE, :] = split_low(lse)
        return carry

    lax.fori_loop(0, PER, one, 0)


def attend(blk, flags, queries, context_keys, span_keys, context_values, span_values):
    steps = queries.shape[0] // TILE
    rows = context_keys.shape[0] + span_keys.shape[0]
    tiles = rows // TILE
    anywhere = pl.BlockSpec(memory_space=pl.ANY)
    return pl.pallas_call(
        attend_kernel,
        out_shape=jax.ShapeDtypeStruct((steps, PIECE, TILE), jnp.bfloat16),
        grid_spec=pltpu.PrefetchScalarGridSpec(
            num_scalar_prefetch=2,
            grid=(steps // PER,),
            in_specs=[pl.BlockSpec((TILE * PER, WIDTH), lambda i, *_: (i, 0))] + [anywhere] * 4,
            out_specs=pl.BlockSpec((PER, PIECE, TILE), lambda i, *_: (i, 0, 0)),
            scratch_shapes=[
                pltpu.VMEM((rows, WIDTH), jnp.bfloat16),
                pltpu.VMEM((rows, WIDTH), jnp.bfloat16),
                pltpu.VMEM((tiles, HEADS * ROWS, TILE), jnp.bfloat16),
                pltpu.VMEM((HEADS, ROWS, TILE), jnp.float32),
                pltpu.VMEM((8, TILE), jnp.float32),
                pltpu.SMEM((tiles,), jnp.int32),
                pltpu.SemaphoreType.DMA((4,)),
            ],
        ),
        compiler_params=pltpu.CompilerParams(vmem_limit_bytes=48 * 1024 * 1024),
        cost_estimate=pl.CostEstimate(flops=6 * 10**9, bytes_accessed=18 * 10**6, transcendentals=12 * 10**6),
    )(blk, flags, queries, context_keys, span_keys, context_values, span_values)


def spread_kernel(
    zs, nq_ref, nk_ref, nv_ref, q_ref, k_ref, v_ref,
    keep_sem, q_send, q_recv, kv_send, kv_recv, own_send, ring_recv, pass_send, far_recv, sib_send, sib_recv,
):
    blk = lax.axis_index("blk")
    uly = lax.axis_index("uly")
    ulys = lax.axis_size("uly")
    z, core = blk // 2, blk % 2
    sibling = {"blk": z * 2 + 1 - core}
    ahead = {"blk": lax.rem(z + 1, zs) * 2 + core}
    behind = {"blk": lax.rem(z + zs - 1, zs) * 2 + core}
    height = nq_ref.shape[0]

    barrier = pltpu.get_barrier_semaphore()
    for d in range(1, ulys):
        pl.semaphore_signal(barrier, inc=1, device_id={"uly": lax.rem(uly + d, ulys)}, device_id_type=MESH)
    for device in (sibling, ahead, behind):
        pl.semaphore_signal(barrier, inc=1, device_id=device, device_id_type=MESH)

    def columns(u):
        return pl.ds(pl.multiple_of(u * WIDTH, WIDTH), WIDTH)

    def span_rows(u):
        return pl.ds(pl.multiple_of(u * height, height), height)

    def q_rows(chip, side, d):
        source = lax.rem(uly + ulys - d, ulys)
        return pl.ds(pl.multiple_of(((chip * 2 + side) * ulys + source) * height, height), height)

    def q_copy(d):
        target = lax.rem(uly + d, ulys)
        return pltpu.make_async_remote_copy(
            src_ref=nq_ref.at[:, columns(target)], dst_ref=q_ref.at[q_rows(z, core, 0), :],
            send_sem=q_send.at[d], recv_sem=q_recv.at[d], device_id={"uly": target}, device_id_type=MESH,
        )

    def kv_copy(which, d):
        target = lax.rem(uly + d, ulys)
        src, dst = ((nk_ref, k_ref), (nv_ref, v_ref))[which]
        return pltpu.make_async_remote_copy(
            src_ref=src.at[:, columns(target)], dst_ref=dst.at[span_rows(uly), :],
            send_sem=kv_send.at[which, d], recv_sem=kv_recv.at[which, d],
            device_id={"uly": target}, device_id_type=MESH,
        )

    def kv_wait(which, d):
        src, dst = ((nk_ref, k_ref), (nv_ref, v_ref))[which]
        return pltpu.make_async_remote_copy(
            src_ref=src.at[:, columns(uly)], dst_ref=dst.at[span_rows(lax.rem(uly + ulys - d, ulys)), :],
            send_sem=kv_send.at[which, d], recv_sem=kv_recv.at[which, d],
            device_id={"uly": lax.rem(uly + d, ulys)}, device_id_type=MESH,
        )

    def move(rows, send, recv, device):
        return pltpu.make_async_remote_copy(
            src_ref=q_ref.at[rows, :], dst_ref=q_ref.at[rows, :],
            send_sem=send, recv_sem=recv, device_id=device, device_id_type=MESH,
        )

    chips = [z, lax.rem(z + zs - 1, zs), lax.rem(z + 1, zs), lax.rem(z + 2, zs)]

    def to_sibling(slot, d):
        return move(q_rows(chips[slot], core, d), sib_send.at[slot, d], sib_recv.at[slot, d], sibling)

    def from_sibling(slot, d):
        return move(q_rows(chips[slot], 1 - core, d), sib_send.at[slot, d], sib_recv.at[slot, d], sibling)

    def to_ring(way, d):
        return move(q_rows(z, core, d), own_send.at[way, d], ring_recv.at[way, d], (ahead, behind)[way])

    def from_ring(way, d):
        return move(q_rows(chips[1 + way], core, d), own_send.at[way, d], ring_recv.at[way, d], (ahead, behind)[way])

    def onward(way, d):
        return move(q_rows(chips[1 + way], core, d), pass_send.at[d], far_recv.at[d], (ahead, behind)[way])

    def from_far(d):
        return move(q_rows(chips[3], core, d), pass_send.at[d], far_recv.at[d], (ahead, behind)[d % 2])

    keeps = [
        pltpu.make_async_copy(nq_ref.at[:, columns(uly)], q_ref.at[q_rows(z, core, 0), :], keep_sem.at[0]),
        pltpu.make_async_copy(nk_ref.at[:, columns(uly)], k_ref.at[span_rows(uly), :], keep_sem.at[1]),
        pltpu.make_async_copy(nv_ref.at[:, columns(uly)], v_ref.at[span_rows(uly), :], keep_sem.at[2]),
    ]
    keeps[0].start()
    pl.semaphore_wait(barrier, ulys - 1 + 3)
    for d in range(1, ulys):
        q_copy(d).start()
    keeps[1].start()
    keeps[2].start()

    for d in range(ulys):
        if d == 0:
            keeps[0].wait()
        else:
            move(q_rows(z, core, d), q_send.at[d], q_recv.at[d], sibling).wait_recv()
        to_ring(0, d).start()
        to_ring(1, d).start()
        to_sibling(0, d).start()
    for which in range(2):
        for d in range(1, ulys):
            kv_copy(which, d).start()
    for d in range(ulys):
        for way in range(2):
            from_ring(way, d).wait_recv()
            if d % 2 == way:
                onward(way, d).start()
            to_sibling(1 + way, d).start()
    for d in range(ulys):
        from_far(d).wait_recv()
        to_sibling(3, d).start()

    for d in range(1, ulys):
        q_copy(d).wait_send()
        for which in range(2):
            kv_copy(which, d).wait_send()
            kv_wait(which, d).wait_recv()
    keeps[1].wait()
    keeps[2].wait()
    for d in range(ulys):
        to_ring(0, d).wait_send()
        to_ring(1, d).wait_send()
        onward(d % 2, d).wait_send()
        for slot in range(4):
            to_sibling(slot, d).wait_send()
            from_sibling(slot, d).wait_recv()


def spread(new_queries, new_keys, new_values, zs, ulys):
    height = new_queries.shape[0]
    dma = pltpu.SemaphoreType.DMA
    anywhere = pl.BlockSpec(memory_space=pl.ANY)
    span = jax.ShapeDtypeStruct((height * ulys, WIDTH), jnp.bfloat16)
    return pl.pallas_call(
        functools.partial(spread_kernel, zs),
        out_shape=(jax.ShapeDtypeStruct((height * ulys * zs * 2, WIDTH), jnp.bfloat16), span, span),
        in_specs=[anywhere] * 3,
        out_specs=(anywhere,) * 3,
        scratch_shapes=[
            dma((3,)), dma((ulys,)), dma((ulys,)),
            dma((2, ulys)), dma((2, ulys)),
            dma((2, ulys)), dma((2, ulys)),
            dma((ulys,)), dma((ulys,)),
            dma((4, ulys)), dma((4, ulys)),
        ],
        compiler_params=pltpu.CompilerParams(
            collective_id=0, has_side_effects=True, vmem_limit_bytes=48 * 1024 * 1024
        ),
        cost_estimate=pl.CostEstimate(flops=0, bytes_accessed=2 * 10**7, transcendentals=0),
    )(new_queries, new_keys, new_values)


def merge(pieces):
    logs = []
    for ref, at in pieces:
        both = ref[at, WIDTH:PIECE, :].astype(jnp.float32)
        logs.append(both[:8] + both[8:])
    best = functools.reduce(jnp.maximum, logs)
    weights = [jnp.exp2(log - best) for log in logs]
    total = functools.reduce(jnp.add, weights)
    inverse = 1.0 / total
    shares = [w * inverse for w in weights]
    return shares, best + jnp.log2(total)


def head_sum(pieces, shares, h):
    found = None
    for (ref, at), share in zip(pieces, shares):
        term = ref[at, h * DH : (h + 1) * DH, :].astype(jnp.float32) * share[h : h + 1, :]
        found = term if found is None else found + term
    return found


def join_kernel(
    zs, part_ref, out_ref, own, sib, far, near, send_far, send_near, done,
    own_sem, sib_send, sib_recv, far_send, far_recv, near_send, near_recv, out_send, out_recv, out_local,
):
    blk = lax.axis_index("blk")
    uly = lax.axis_index("uly")
    z, core = blk // 2, blk % 2
    ring = [lax.rem(z + d, zs) for d in (2, 1, zs - 1, 0)]
    sibling = {"blk": z * 2 + 1 - core}
    ahead = {"blk": ring[1] * 2 + core}
    behind = {"blk": ring[2] * 2 + core}
    ulys = lax.axis_size("uly")
    tiles = own.shape[1]

    barrier = pltpu.get_barrier_semaphore()
    for device in (sibling, ahead, behind):
        pl.semaphore_signal(barrier, inc=1, device_id=device, device_id_type=MESH)
    for d in range(1, ulys):
        pl.semaphore_signal(barrier, inc=1, device_id={"uly": lax.rem(uly + d, ulys)}, device_id_type=MESH)

    def own_copy(slot, t):
        index = (ring[slot] * 2 + core) * tiles + t
        return pltpu.make_async_copy(part_ref.at[index], own.at[slot, t], own_sem.at[slot, t])

    def sib_copy(slot, t):
        index = (ring[slot] * 2 + 1 - core) * tiles + t
        return pltpu.make_async_remote_copy(
            src_ref=part_ref.at[index], dst_ref=sib.at[slot, t],
            send_sem=sib_send.at[slot, t], recv_sem=sib_recv.at[slot, t],
            device_id=sibling, device_id_type=MESH,
        )

    def far_copy(t):
        return pltpu.make_async_remote_copy(
            src_ref=send_far.at[t], dst_ref=far.at[t],
            send_sem=far_send.at[t], recv_sem=far_recv.at[t],
            device_id=ahead if t < 2 else behind, device_id_type=MESH,
        )

    def near_copy(way, t):
        return pltpu.make_async_remote_copy(
            src_ref=send_near.at[way, t], dst_ref=near.at[way, t],
            send_sem=near_send.at[way, t], recv_sem=near_recv.at[way, t],
            device_id=ahead if way == 0 else behind, device_id_type=MESH,
        )

    order = (
        [(0, 0), (0, 2), (0, 1), (0, 3), (1, 2), (2, 0), (1, 3), (2, 1), (1, 0), (2, 2), (1, 1), (2, 3)]
        + [(3, 0), (3, 2), (3, 1), (3, 3)]
    )
    for slot, t in order:
        own_copy(slot, t).start()
    pl.semaphore_wait(barrier, 3 + ulys - 1)
    for slot, t in order:
        sib_copy(slot, t).start()

    def ready(slot, t):
        own_copy(slot, t).wait()
        sib_copy(slot, t).wait_recv()
        return [(own.at[slot], t), (sib.at[slot], t)]

    def store(pieces, dst):
        shares, log = merge(pieces)
        for h in range(HEADS):
            dst[h * DH : (h + 1) * DH, :] = head_sum(pieces, shares, h).astype(jnp.bfloat16)
        dst[WIDTH:PIECE, :] = split_low(log)

    for t in (0, 2, 1, 3):
        store(ready(0, t), send_far.at[t])
        far_copy(t).start()
    for way, t in ((0, 2), (1, 0), (0, 3), (1, 1)):
        store(ready(way + 1, t), send_near.at[way, t])
        near_copy(way, t).start()
    for way, t in ((0, 0), (1, 2), (0, 1), (1, 3)):
        pieces = ready(way + 1, t)
        far_copy(t).wait_recv()
        store(pieces + [(far, t)], send_near.at[way, t])
        near_copy(way, t).start()

    half = out_ref.shape[0]

    def out_copy(u):
        return pltpu.make_async_remote_copy(
            src_ref=done.at[u], dst_ref=out_ref.at[:, pl.ds(pl.multiple_of(uly * WIDTH, WIDTH), WIDTH)],
            send_sem=out_send.at[u], recv_sem=out_recv.at[uly],
            device_id={"uly": u}, device_id_type=MESH,
        )

    def out_keep(u):
        return pltpu.make_async_copy(
            done.at[u], out_ref.at[:, pl.ds(pl.multiple_of(uly * WIDTH, WIDTH), WIDTH)], out_local
        )

    for t in (0, 2, 1, 3):
        pieces = ready(3, t)
        near_copy(0, t).wait_recv()
        near_copy(1, t).wait_recv()
        pieces = pieces + [(near.at[0], t), (near.at[1], t)]
        shares, log = merge(pieces)
        for h in range(HEADS):
            flat = head_sum(pieces, shares, h).astype(jnp.bfloat16).T
            for j in range(2):
                done[2 * t + j, :, h * DH : (h + 1) * DH] = flat[j * half : (j + 1) * half]
        for j in range(2):
            u = 2 * t + j

            @pl.when(uly != u)
            def _():
                out_copy(u).start()

            @pl.when(uly == u)
            def _():
                out_keep(u).start()

    out_keep(0).wait()
    for u in range(ulys):

        @pl.when(uly != u)
        def _():
            pltpu.make_async_remote_copy(
                src_ref=done.at[u], dst_ref=out_ref.at[:, u * WIDTH : (u + 1) * WIDTH],
                send_sem=out_send.at[u], recv_sem=out_recv.at[u],
                device_id={"uly": u}, device_id_type=MESH,
            ).wait()

    for slot, t in order:
        sib_copy(slot, t).wait_send()
    for t in range(tiles):
        far_copy(t).wait_send()
        near_copy(0, t).wait_send()
        near_copy(1, t).wait_send()


def join(part, rows, zs, ulys):
    tiles = part.shape[0] // (2 * zs)
    piece = (PIECE, TILE)
    dma = pltpu.SemaphoreType.DMA
    return pl.pallas_call(
        functools.partial(join_kernel, zs),
        out_shape=jax.ShapeDtypeStruct((rows, ulys * WIDTH), jnp.bfloat16),
        in_specs=[pl.BlockSpec(memory_space=pl.ANY)],
        out_specs=pl.BlockSpec(memory_space=pl.ANY),
        scratch_shapes=[
            pltpu.VMEM((4, tiles) + piece, jnp.bfloat16),
            pltpu.VMEM((4, tiles) + piece, jnp.bfloat16),
            pltpu.VMEM((tiles,) + piece, jnp.bfloat16),
            pltpu.VMEM((2, tiles) + piece, jnp.bfloat16),
            pltpu.VMEM((tiles,) + piece, jnp.bfloat16),
            pltpu.VMEM((2, tiles) + piece, jnp.bfloat16),
            pltpu.VMEM((ulys, rows, WIDTH), jnp.bfloat16),
            dma((4, tiles)), dma((4, tiles)), dma((4, tiles)),
            dma((tiles,)), dma((tiles,)),
            dma((2, tiles)), dma((2, tiles)),
            dma((ulys,)), dma((ulys,)), dma,
        ],
        compiler_params=pltpu.CompilerParams(
            collective_id=1, has_side_effects=True, vmem_limit_bytes=48 * 1024 * 1024
        ),
        cost_estimate=pl.CostEstimate(flops=2 * 10**7, bytes_accessed=10**7, transcendentals=10**5),
    )(part)


def shards(new_queries, new_keys, new_values, context_keys, context_values, keep_flags):
    zs, ulys = lax.axis_size("blk") // 2, lax.axis_size("uly")
    queries, span_keys, span_values = spread(new_queries, new_keys, new_values, zs, ulys)
    blk = jnp.reshape(lax.axis_index("blk").astype(jnp.int32), (1,))
    part = attend(blk, keep_flags, queries, context_keys, span_keys, context_values, span_values)
    return join(part, new_queries.shape[0], zs, ulys)


def solution(mesh):
    in_specs = (
        P(("cfg", "blk", "uly"), None),
        P(("cfg", "blk", "uly"), None),
        P(("cfg", "blk", "uly"), None),
        P(("cfg", "blk"), "uly"),
        P(("cfg", "blk"), "uly"),
        P(),
    )
    out_specs = P(("cfg", "blk", "uly"), None)
    return jax.shard_map(shards, mesh=mesh, in_specs=in_specs, out_specs=out_specs, check_vma=False)
```

```python
import functools

import jax
import jax.numpy as jnp
from jax import lax
from jax.experimental import pallas as pl
from jax.experimental.pallas import tpu as pltpu
from jax.sharding import PartitionSpec as P

DH = 128
TILE = 128
HEADS = 6
WIDTH = HEADS * DH
ROWS = 144
PIECE = WIDTH + 16
GROUP = 4
PER = 4
VMEM_LIMIT = 62 * 1024 * 1024
DEPTH = 1
LOW = -1e30
LOG2 = 1.4426950408889634 * DH ** (-0.5)
MESH = pl.DeviceIdType.MESH


def split_low(x):
    high = x.astype(jnp.bfloat16).astype(jnp.float32)
    return jnp.concatenate([high, x - high], axis=0).astype(jnp.bfloat16)


def attend_kernel(
    blk_ref, flags_ref, q_ref, ck_ref, sk_ref, cv_ref, sv_ref, o_ref, k_ref, v_ref, vt, acc, top, order_ref, sems
):
    step = pl.program_id(0)
    tiles = vt.shape[0]
    ctx_rows = ck_ref.shape[0]
    ctx_tiles = ctx_rows // TILE
    span_tiles = tiles - ctx_tiles
    blk = blk_ref[0]
    first_span = flags_ref.shape[1] - flags_ref.shape[0]

    @pl.when(step == 0)
    def _():
        copies = [
            pltpu.make_async_copy(cv_ref, v_ref.at[:ctx_rows], sems.at[0]),
            pltpu.make_async_copy(sv_ref, v_ref.at[ctx_rows:], sems.at[1]),
            pltpu.make_async_copy(ck_ref, k_ref.at[:ctx_rows], sems.at[2]),
            pltpu.make_async_copy(sk_ref, k_ref.at[ctx_rows:], sems.at[3]),
        ]
        for copy in copies:
            copy.start()
        copies[0].wait()
        copies[1].wait()

        def turn(t, carry):
            rows = pl.ds(pl.multiple_of(t * TILE, TILE), TILE)
            for h in range(HEADS):
                vt[t, h * ROWS : h * ROWS + DH, :] = v_ref[rows, h * DH : (h + 1) * DH].T
                vt[t, h * ROWS + DH : (h + 1) * ROWS, :] = jnp.ones((ROWS - DH, TILE), jnp.bfloat16)
            return carry

        lax.fori_loop(0, tiles, turn, 0)
        top[...] = jnp.full_like(top, LOW)
        copies[2].wait()
        copies[3].wait()

    def one(sub, carry):
        tile = step * PER + sub
        q_rows = pl.ds(pl.multiple_of(sub * TILE, TILE), TILE)
        count = jnp.int32(0)
        for t in range(tiles):
            column = blk * ctx_tiles + t if t < ctx_tiles else first_span + blk * span_tiles + t - ctx_tiles
            order_ref[count] = t
            count = count + jnp.where(flags_ref[tile, column] > 0, 1, 0)

        def scores(h, picked):
            cols = slice(h * DH, (h + 1) * DH)
            ks = [k_ref[pl.ds(pl.multiple_of(t * TILE, TILE), TILE), cols] for t in picked]
            return lax.dot_general(
                jnp.concatenate(ks, axis=0),
                q_ref[q_rows, cols],
                (((1,), (1,)), ((), ())),
                preferred_element_type=jnp.float32,
            )

        def weigh(h, picked, s, first):
            new = jnp.max(s, axis=0, keepdims=True)
            if not first:
                old = top[h : h + 1, :]
                new = jnp.maximum(old, new)
                scale = jnp.exp2((old - new) * LOG2)
            top[h : h + 1, :] = new
            p = jnp.exp2((s - new) * LOG2).astype(jnp.bfloat16)
            vs = jnp.concatenate([vt[t, h * ROWS : (h + 1) * ROWS, :] for t in picked], axis=1)
            got = jnp.dot(vs, p, preferred_element_type=jnp.float32)
            acc[h] = got if first else acc[h] * scale + got

        def visit(picked, first):
            all_scores = [scores(h, picked) for h in range(HEADS)]
            for h in range(HEADS):
                weigh(h, picked, all_scores[h], first)

        def none():
            acc[...] = jnp.zeros_like(acc)

        def lead_visit(n):
            visit([order_ref[a] for a in range(n)], True)

        lead = jnp.where(count == 0, 0, lax.rem(count + GROUP - 1, GROUP) + 1)
        lax.switch(lead, [none] + [functools.partial(lead_visit, n) for n in range(1, GROUP + 1)])

        def more(j, inner):
            visit([order_ref[lead + GROUP * j + a] for a in range(GROUP)], False)
            return inner

        lax.fori_loop(0, (count - lead) // GROUP, more, 0)

        totals = [acc[h, DH : DH + 1, :] for h in range(HEADS)]
        for h in range(HEADS):
            safe = jnp.where(totals[h] > 0, totals[h], 1.0)
            o_ref[sub, h * DH : (h + 1) * DH, :] = (acc[h, :DH, :] * (1.0 / safe)).astype(jnp.bfloat16)
        total = jnp.concatenate(totals + [jnp.zeros((8 - HEADS, TILE), jnp.float32)], axis=0)
        found = total > 0
        lse = jnp.where(found, top[...] * LOG2 + jnp.log2(jnp.where(found, total, 1.0)), LOW)
        o_ref[sub, WIDTH:PIECE, :] = split_low(lse)
        return carry

    lax.fori_loop(0, PER, one, 0)


def attend(blk, flags, queries, context_keys, span_keys, context_values, span_values):
    steps = queries.shape[0] // TILE
    rows = context_keys.shape[0] + span_keys.shape[0]
    tiles = rows // TILE
    anywhere = pl.BlockSpec(memory_space=pl.ANY)
    return pl.pallas_call(
        attend_kernel,
        out_shape=jax.ShapeDtypeStruct((steps, PIECE, TILE), jnp.bfloat16),
        grid_spec=pltpu.PrefetchScalarGridSpec(
            num_scalar_prefetch=2,
            grid=(steps // PER,),
            in_specs=[pl.BlockSpec((TILE * PER, WIDTH), lambda i, *_: (i, 0))] + [anywhere] * 4,
            out_specs=pl.BlockSpec((PER, PIECE, TILE), lambda i, *_: (i, 0, 0)),
            scratch_shapes=[
                pltpu.VMEM((rows, WIDTH), jnp.bfloat16),
                pltpu.VMEM((rows, WIDTH), jnp.bfloat16),
                pltpu.VMEM((tiles, HEADS * ROWS, TILE), jnp.bfloat16),
                pltpu.VMEM((HEADS, ROWS, TILE), jnp.float32),
                pltpu.VMEM((8, TILE), jnp.float32),
                pltpu.SMEM((tiles,), jnp.int32),
                pltpu.SemaphoreType.DMA((4,)),
            ],
        ),
        compiler_params=pltpu.CompilerParams(vmem_limit_bytes=VMEM_LIMIT),
        cost_estimate=pl.CostEstimate(flops=6 * 10**9, bytes_accessed=18 * 10**6, transcendentals=12 * 10**6),
    )(blk, flags, queries, context_keys, span_keys, context_values, span_values)


def spread_kernel(
    zs, nq_ref, nk_ref, nv_ref, q_ref, k_ref, v_ref, stage,
    keep_sem, q_send, q_recv, kv_send, kv_recv, own_send, ring_recv, pass_send, far_recv, sib_send, sib_recv,
):
    blk = lax.axis_index("blk")
    uly = lax.axis_index("uly")
    ulys = lax.axis_size("uly")
    z, core = blk // 2, blk % 2
    sibling = {"blk": z * 2 + 1 - core}
    ahead = {"blk": lax.rem(z + 1, zs) * 2 + core}
    behind = {"blk": lax.rem(z + zs - 1, zs) * 2 + core}
    height = nq_ref.shape[0]

    barrier = pltpu.get_barrier_semaphore()
    for d in range(1, ulys):
        pl.semaphore_signal(barrier, inc=1, device_id={"uly": lax.rem(uly + d, ulys)}, device_id_type=MESH)
    for device in (sibling, ahead, behind):
        pl.semaphore_signal(barrier, inc=1, device_id=device, device_id_type=MESH)

    def columns(u):
        return pl.ds(pl.multiple_of(u * WIDTH, WIDTH), WIDTH)

    def span_rows(u):
        return pl.ds(pl.multiple_of(u * height, height), height)

    def q_rows(chip, side, d):
        source = lax.rem(uly + ulys - d, ulys)
        return pl.ds(pl.multiple_of(((chip * 2 + side) * ulys + source) * height, height), height)

    def q_copy(d):
        target = lax.rem(uly + d, ulys)
        return pltpu.make_async_remote_copy(
            src_ref=nq_ref.at[:, columns(target)], dst_ref=q_ref.at[q_rows(z, core, 0), :],
            send_sem=q_send.at[d], recv_sem=q_recv.at[d], device_id={"uly": target}, device_id_type=MESH,
        )

    def kv_copy(which, d):
        target = lax.rem(uly + d, ulys)
        src, dst = ((nk_ref, k_ref), (nv_ref, v_ref))[which]
        return pltpu.make_async_remote_copy(
            src_ref=src.at[:, columns(target)], dst_ref=dst.at[span_rows(uly), :],
            send_sem=kv_send.at[which, d], recv_sem=kv_recv.at[which, d],
            device_id={"uly": target}, device_id_type=MESH,
        )

    def kv_wait(which, d):
        src, dst = ((nk_ref, k_ref), (nv_ref, v_ref))[which]
        return pltpu.make_async_remote_copy(
            src_ref=src.at[:, columns(uly)], dst_ref=dst.at[span_rows(lax.rem(uly + ulys - d, ulys)), :],
            send_sem=kv_send.at[which, d], recv_sem=kv_recv.at[which, d],
            device_id={"uly": lax.rem(uly + d, ulys)}, device_id_type=MESH,
        )

    def move(rows, send, recv, device):
        return pltpu.make_async_remote_copy(
            src_ref=q_ref.at[rows, :], dst_ref=q_ref.at[rows, :],
            send_sem=send, recv_sem=recv, device_id=device, device_id_type=MESH,
        )

    chips = [z, lax.rem(z + zs - 1, zs), lax.rem(z + 1, zs), lax.rem(z + 2, zs)]

    def to_sibling(slot, d):
        return move(q_rows(chips[slot], core, d), sib_send.at[slot, d], sib_recv.at[slot, d], sibling)

    def from_sibling(slot, d):
        return move(q_rows(chips[slot], 1 - core, d), sib_send.at[slot, d], sib_recv.at[slot, d], sibling)

    def to_ring(way, d):
        return move(q_rows(z, core, d), own_send.at[way, d], ring_recv.at[way, d], (ahead, behind)[way])

    def from_ring(way, d):
        return move(q_rows(chips[1 + way], core, d), own_send.at[way, d], ring_recv.at[way, d], (ahead, behind)[way])

    def onward(way, d):
        return move(q_rows(chips[1 + way], core, d), pass_send.at[d], far_recv.at[d], (ahead, behind)[way])

    def from_far(d):
        return move(q_rows(chips[3], core, d), pass_send.at[d], far_recv.at[d], (ahead, behind)[d % 2])

    fetches = [
        pltpu.make_async_copy(src.at[:, columns(uly)], stage.at[i], keep_sem.at[i])
        for i, src in enumerate((nq_ref, nk_ref, nv_ref))
    ]
    keeps = [
        pltpu.make_async_copy(stage.at[i], dst, keep_sem.at[i])
        for i, dst in enumerate(
            (q_ref.at[q_rows(z, core, 0), :], k_ref.at[span_rows(uly), :], v_ref.at[span_rows(uly), :])
        )
    ]
    for fetch in fetches:
        fetch.start()
    for fetch in fetches:
        fetch.wait()
    pl.semaphore_wait(barrier, ulys - 1 + 3)

    def own_piece(send, recv, device):
        return pltpu.make_async_remote_copy(
            src_ref=stage.at[0], dst_ref=q_ref.at[q_rows(z, core, 0), :],
            send_sem=send, recv_sem=recv, device_id=device, device_id_type=MESH,
        )

    own_piece(own_send.at[0, 0], ring_recv.at[0, 0], ahead).start()
    own_piece(own_send.at[1, 0], ring_recv.at[1, 0], behind).start()
    for d in range(1, ulys):
        q_copy(d).start()
    own_piece(sib_send.at[0, 0], sib_recv.at[0, 0], sibling).start()
    for keep in keeps:
        keep.start()

    for d in range(1, ulys):
        move(q_rows(z, core, d), q_send.at[d], q_recv.at[d], sibling).wait_recv()
        to_ring(0, d).start()
        to_ring(1, d).start()
        to_sibling(0, d).start()
    for which in range(2):
        for d in range(1, ulys):
            kv_copy(which, d).start()
    for d in range(ulys):
        for way in range(2):
            from_ring(way, d).wait_recv()
            if d % 2 == way:
                onward(way, d).start()
            to_sibling(1 + way, d).start()
    for d in range(ulys):
        from_far(d).wait_recv()
        to_sibling(3, d).start()

    for d in range(1, ulys):
        q_copy(d).wait_send()
        for which in range(2):
            kv_copy(which, d).wait_send()
            kv_wait(which, d).wait_recv()
    for keep in keeps:
        keep.wait()
    for d in range(ulys):
        to_ring(0, d).wait_send()
        to_ring(1, d).wait_send()
        onward(d % 2, d).wait_send()
        for slot in range(4):
            to_sibling(slot, d).wait_send()
            from_sibling(slot, d).wait_recv()


def spread(new_queries, new_keys, new_values, zs, ulys):
    height = new_queries.shape[0]
    dma = pltpu.SemaphoreType.DMA
    anywhere = pl.BlockSpec(memory_space=pl.ANY)
    span = jax.ShapeDtypeStruct((height * ulys, WIDTH), jnp.bfloat16)
    return pl.pallas_call(
        functools.partial(spread_kernel, zs),
        out_shape=(jax.ShapeDtypeStruct((height * ulys * zs * 2, WIDTH), jnp.bfloat16), span, span),
        in_specs=[pl.BlockSpec(memory_space=pltpu.HBM)] * 3,
        out_specs=(anywhere,) * 3,
        scratch_shapes=[
            pltpu.VMEM((3, height, WIDTH), jnp.bfloat16),
            dma((3,)), dma((ulys,)), dma((ulys,)),
            dma((2, ulys)), dma((2, ulys)),
            dma((2, ulys)), dma((2, ulys)),
            dma((ulys,)), dma((ulys,)),
            dma((4, ulys)), dma((4, ulys)),
        ],
        compiler_params=pltpu.CompilerParams(
            collective_id=0, has_side_effects=True, vmem_limit_bytes=VMEM_LIMIT
        ),
        cost_estimate=pl.CostEstimate(flops=0, bytes_accessed=2 * 10**7, transcendentals=0),
    )(new_queries, new_keys, new_values)


def merge(pieces):
    logs = []
    for ref, at in pieces:
        both = ref[at, WIDTH:PIECE, :].astype(jnp.float32)
        logs.append(both[:8] + both[8:])
    best = functools.reduce(jnp.maximum, logs)
    weights = [jnp.exp2(log - best) for log in logs]
    total = functools.reduce(jnp.add, weights)
    inverse = 1.0 / total
    shares = [w * inverse for w in weights]
    return shares, best + jnp.log2(total)


def head_sum(pieces, shares, h):
    found = None
    for (ref, at), share in zip(pieces, shares):
        term = ref[at, h * DH : (h + 1) * DH, :].astype(jnp.float32) * share[h : h + 1, :]
        found = term if found is None else found + term
    return found


def join_kernel(
    zs, part_ref, out_ref, own, sib, far, near, send_far, send_near, done,
    own_sem, sib_send, sib_recv, far_send, far_recv, near_send, near_recv, out_send, out_recv, out_local,
):
    blk = lax.axis_index("blk")
    uly = lax.axis_index("uly")
    z, core = blk // 2, blk % 2
    ring = [lax.rem(z + d, zs) for d in (2, 1, zs - 1, 0)]
    sibling = {"blk": z * 2 + 1 - core}
    ahead = {"blk": ring[1] * 2 + core}
    behind = {"blk": ring[2] * 2 + core}
    ulys = lax.axis_size("uly")
    tiles = own.shape[1]

    barrier = pltpu.get_barrier_semaphore()
    for device in (sibling, ahead, behind):
        pl.semaphore_signal(barrier, inc=1, device_id=device, device_id_type=MESH)
    for d in range(1, ulys):
        pl.semaphore_signal(barrier, inc=1, device_id={"uly": lax.rem(uly + d, ulys)}, device_id_type=MESH)

    def turned(t):
        return lax.rem(t + uly, tiles)

    def own_copy(slot, t):
        index = (ring[slot] * 2 + core) * tiles + turned(t)
        return pltpu.make_async_copy(part_ref.at[index], own.at[slot, t], own_sem.at[slot, t])

    def sib_copy(slot, t):
        index = (ring[slot] * 2 + 1 - core) * tiles + turned(t)
        return pltpu.make_async_remote_copy(
            src_ref=part_ref.at[index], dst_ref=sib.at[slot, t],
            send_sem=sib_send.at[slot, t], recv_sem=sib_recv.at[slot, t],
            device_id=sibling, device_id_type=MESH,
        )

    def far_copy(t):
        return pltpu.make_async_remote_copy(
            src_ref=send_far.at[t], dst_ref=far.at[t],
            send_sem=far_send.at[t], recv_sem=far_recv.at[t],
            device_id=ahead if t < 2 else behind, device_id_type=MESH,
        )

    def near_copy(way, t):
        return pltpu.make_async_remote_copy(
            src_ref=send_near.at[way, t], dst_ref=near.at[way, t],
            send_sem=near_send.at[way, t], recv_sem=near_recv.at[way, t],
            device_id=ahead if way == 0 else behind, device_id_type=MESH,
        )

    order = [(0, 0), (0, 2), (0, 1), (0, 3)]
    order += [(slot, t) for t in (0, 2, 1, 3) for slot in (1, 2)]
    order += [(3, t) for t in (0, 2, 1, 3)]
    for slot, t in order:
        own_copy(slot, t).start()
    pl.semaphore_wait(barrier, 3 + ulys - 1)
    for slot, t in order:
        sib_copy(slot, t).start()

    def ready(slot, t):
        own_copy(slot, t).wait()
        sib_copy(slot, t).wait_recv()
        return [(own.at[slot], t), (sib.at[slot], t)]

    def store(pieces, dst):
        shares, log = merge(pieces)
        for h in range(HEADS):
            dst[h * DH : (h + 1) * DH, :] = head_sum(pieces, shares, h).astype(jnp.bfloat16)
        dst[WIDTH:PIECE, :] = split_low(log)

    for t in (0, 2, 1, 3):
        store(ready(0, t), send_far.at[t])
        far_copy(t).start()
    for t in (0, 2, 1, 3):
        passed = t // 2
        for way in (1 - passed, passed):
            pieces = ready(way + 1, t)
            if way == passed:
                far_copy(t).wait_recv()
                pieces = pieces + [(far, t)]
            place = (0, 2, 1, 3).index(t)
            store(pieces, send_near.at[way, t])
            if place >= DEPTH:
                near_copy(way, (0, 2, 1, 3)[place - DEPTH]).wait_send()
            near_copy(way, t).start()

    half = out_ref.shape[0]

    def out_copy(i, u):
        return pltpu.make_async_remote_copy(
            src_ref=done.at[i], dst_ref=out_ref.at[:, pl.ds(pl.multiple_of(uly * WIDTH, WIDTH), WIDTH)],
            send_sem=out_send.at[i], recv_sem=out_recv.at[uly],
            device_id={"uly": u}, device_id_type=MESH,
        )

    def out_keep(i):
        return pltpu.make_async_copy(
            done.at[i], out_ref.at[:, pl.ds(pl.multiple_of(uly * WIDTH, WIDTH), WIDTH)], out_local
        )

    for t in (0, 2, 1, 3):
        pieces = ready(3, t)
        near_copy(0, t).wait_recv()
        near_copy(1, t).wait_recv()
        pieces = pieces + [(near.at[0], t), (near.at[1], t)]
        shares, log = merge(pieces)
        for h in range(HEADS):
            flat = head_sum(pieces, shares, h).astype(jnp.bfloat16).T
            for j in range(2):
                done[2 * t + j, :, h * DH : (h + 1) * DH] = flat[j * half : (j + 1) * half]
        for j in range(2):
            u = 2 * turned(t) + j

            @pl.when(uly != u)
            def _():
                out_copy(2 * t + j, u).start()

            @pl.when(uly == u)
            def _():
                out_keep(2 * t + j).start()

    out_keep(0).wait()
    for i in range(ulys):
        u = 2 * turned(i // 2) + i % 2

        @pl.when(uly != u)
        def _():
            out_copy(i, u).wait_send()
            pltpu.make_async_remote_copy(
                src_ref=done.at[i], dst_ref=out_ref.at[:, pl.ds(pl.multiple_of(u * WIDTH, WIDTH), WIDTH)],
                send_sem=out_send.at[i], recv_sem=out_recv.at[u],
                device_id={"uly": u}, device_id_type=MESH,
            ).wait_recv()

    for slot, t in order:
        sib_copy(slot, t).wait_send()
    for t in range(tiles):
        far_copy(t).wait_send()
        if (0, 2, 1, 3).index(t) >= tiles - DEPTH:
            near_copy(0, t).wait_send()
            near_copy(1, t).wait_send()


def join(part, rows, zs, ulys):
    tiles = part.shape[0] // (2 * zs)
    piece = (PIECE, TILE)
    dma = pltpu.SemaphoreType.DMA
    return pl.pallas_call(
        functools.partial(join_kernel, zs),
        out_shape=jax.ShapeDtypeStruct((rows, ulys * WIDTH), jnp.bfloat16),
        in_specs=[pl.BlockSpec(memory_space=pl.ANY)],
        out_specs=pl.BlockSpec(memory_space=pl.ANY),
        scratch_shapes=[
            pltpu.VMEM((4, tiles) + piece, jnp.bfloat16),
            pltpu.VMEM((4, tiles) + piece, jnp.bfloat16),
            pltpu.VMEM((tiles,) + piece, jnp.bfloat16),
            pltpu.VMEM((2, tiles) + piece, jnp.bfloat16),
            pltpu.VMEM((tiles,) + piece, jnp.bfloat16),
            pltpu.VMEM((2, tiles) + piece, jnp.bfloat16),
            pltpu.VMEM((ulys, rows, WIDTH), jnp.bfloat16),
            dma((4, tiles)), dma((4, tiles)), dma((4, tiles)),
            dma((tiles,)), dma((tiles,)),
            dma((2, tiles)), dma((2, tiles)),
            dma((ulys,)), dma((ulys,)), dma,
        ],
        compiler_params=pltpu.CompilerParams(
            collective_id=1, has_side_effects=True, vmem_limit_bytes=VMEM_LIMIT
        ),
        cost_estimate=pl.CostEstimate(flops=2 * 10**7, bytes_accessed=10**7, transcendentals=10**5),
    )(part)


def shards(new_queries, new_keys, new_values, context_keys, context_values, keep_flags):
    zs, ulys = lax.axis_size("blk") // 2, lax.axis_size("uly")
    queries, span_keys, span_values = spread(new_queries, new_keys, new_values, zs, ulys)
    blk = jnp.reshape(lax.axis_index("blk").astype(jnp.int32), (1,))
    part = attend(blk, keep_flags, queries, context_keys, span_keys, context_values, span_values)
    return join(part, new_queries.shape[0], zs, ulys)


def solution(mesh):
    in_specs = (
        P(("cfg", "blk", "uly"), None),
        P(("cfg", "blk", "uly"), None),
        P(("cfg", "blk", "uly"), None),
        P(("cfg", "blk"), "uly"),
        P(("cfg", "blk"), "uly"),
        P(),
    )
    out_specs = P(("cfg", "blk", "uly"), None)
    return jax.shard_map(shards, mesh=mesh, in_specs=in_specs, out_specs=out_specs, check_vma=False)
```

```python
import functools

import jax
import jax.numpy as jnp
from jax import lax
from jax.experimental import pallas as pl
from jax.experimental.pallas import tpu as pltpu
from jax.sharding import PartitionSpec as P

DH = 128
TILE = 128
HEADS = 6
WIDTH = HEADS * DH
ROWS = 144
PIECE = WIDTH + 16
GROUP = 4
PER = 4
VMEM_LIMIT = 62 * 1024 * 1024
FLIGHT = 7
DEPTH = 1
LOW = -1e30
LOG2 = 1.4426950408889634 * DH ** (-0.5)
MESH = pl.DeviceIdType.MESH


def split_low(x):
    high = x.astype(jnp.bfloat16).astype(jnp.float32)
    return jnp.concatenate([high, x - high], axis=0).astype(jnp.bfloat16)


def attend_kernel(
    blk_ref, flags_ref, q_ref, ck_ref, sk_ref, cv_ref, sv_ref, o_ref, k_ref, v_ref, vt, acc, top, order_ref, sems
):
    step = pl.program_id(0)
    tiles = vt.shape[0]
    ctx_rows = ck_ref.shape[0]
    ctx_tiles = ctx_rows // TILE
    span_tiles = tiles - ctx_tiles
    blk = blk_ref[0]
    first_span = flags_ref.shape[1] - flags_ref.shape[0]

    @pl.when(step == 0)
    def _():
        copies = [
            pltpu.make_async_copy(cv_ref, v_ref.at[:ctx_rows], sems.at[0]),
            pltpu.make_async_copy(sv_ref, v_ref.at[ctx_rows:], sems.at[1]),
            pltpu.make_async_copy(ck_ref, k_ref.at[:ctx_rows], sems.at[2]),
            pltpu.make_async_copy(sk_ref, k_ref.at[ctx_rows:], sems.at[3]),
        ]
        for copy in copies:
            copy.start()
        copies[0].wait()
        copies[1].wait()

        def turn(t, carry):
            rows = pl.ds(pl.multiple_of(t * TILE, TILE), TILE)
            for h in range(HEADS):
                vt[t, h * ROWS : h * ROWS + DH, :] = v_ref[rows, h * DH : (h + 1) * DH].T
                vt[t, h * ROWS + DH : (h + 1) * ROWS, :] = jnp.ones((ROWS - DH, TILE), jnp.bfloat16)
            return carry

        lax.fori_loop(0, tiles, turn, 0)
        top[...] = jnp.full_like(top, LOW)
        copies[2].wait()
        copies[3].wait()

    def one(sub, carry):
        tile = step * PER + sub
        q_rows = pl.ds(pl.multiple_of(sub * TILE, TILE), TILE)
        count = jnp.int32(0)
        for t in range(tiles):
            column = blk * ctx_tiles + t if t < ctx_tiles else first_span + blk * span_tiles + t - ctx_tiles
            order_ref[count] = t
            count = count + jnp.where(flags_ref[tile, column] > 0, 1, 0)

        def scores(h, picked):
            cols = slice(h * DH, (h + 1) * DH)
            ks = [k_ref[pl.ds(pl.multiple_of(t * TILE, TILE), TILE), cols] for t in picked]
            return lax.dot_general(
                jnp.concatenate(ks, axis=0),
                q_ref[q_rows, cols],
                (((1,), (1,)), ((), ())),
                preferred_element_type=jnp.float32,
            )

        def weigh(h, picked, s, first):
            new = jnp.max(s, axis=0, keepdims=True)
            if not first:
                old = top[h : h + 1, :]
                new = jnp.maximum(old, new)
                scale = jnp.exp2((old - new) * LOG2)
            top[h : h + 1, :] = new
            p = jnp.exp2((s - new) * LOG2).astype(jnp.bfloat16)
            vs = jnp.concatenate([vt[t, h * ROWS : (h + 1) * ROWS, :] for t in picked], axis=1)
            got = jnp.dot(vs, p, preferred_element_type=jnp.float32)
            acc[h] = got if first else acc[h] * scale + got

        def visit(picked, first):
            all_scores = [scores(h, picked) for h in range(HEADS)]
            for h in range(HEADS):
                weigh(h, picked, all_scores[h], first)

        def none():
            acc[...] = jnp.zeros_like(acc)

        def lead_visit(n):
            visit([order_ref[a] for a in range(n)], True)

        lead = jnp.where(count == 0, 0, lax.rem(count + GROUP - 1, GROUP) + 1)
        lax.switch(lead, [none] + [functools.partial(lead_visit, n) for n in range(1, GROUP + 1)])

        def more(j, inner):
            visit([order_ref[lead + GROUP * j + a] for a in range(GROUP)], False)
            return inner

        lax.fori_loop(0, (count - lead) // GROUP, more, 0)

        totals = [acc[h, DH : DH + 1, :] for h in range(HEADS)]
        for h in range(HEADS):
            safe = jnp.where(totals[h] > 0, totals[h], 1.0)
            o_ref[sub, h * DH : (h + 1) * DH, :] = (acc[h, :DH, :] * (1.0 / safe)).astype(jnp.bfloat16)
        total = jnp.concatenate(totals + [jnp.zeros((8 - HEADS, TILE), jnp.float32)], axis=0)
        found = total > 0
        lse = jnp.where(found, top[...] * LOG2 + jnp.log2(jnp.where(found, total, 1.0)), LOW)
        o_ref[sub, WIDTH:PIECE, :] = split_low(lse)
        return carry

    lax.fori_loop(0, PER, one, 0)


def attend(blk, flags, queries, context_keys, span_keys, context_values, span_values):
    steps = queries.shape[0] // TILE
    rows = context_keys.shape[0] + span_keys.shape[0]
    tiles = rows // TILE
    anywhere = pl.BlockSpec(memory_space=pl.ANY)
    return pl.pallas_call(
        attend_kernel,
        out_shape=jax.ShapeDtypeStruct((steps, PIECE, TILE), jnp.bfloat16),
        grid_spec=pltpu.PrefetchScalarGridSpec(
            num_scalar_prefetch=2,
            grid=(steps // PER,),
            in_specs=[pl.BlockSpec((TILE * PER, WIDTH), lambda i, *_: (i, 0))] + [anywhere] * 4,
            out_specs=pl.BlockSpec((PER, PIECE, TILE), lambda i, *_: (i, 0, 0)),
            scratch_shapes=[
                pltpu.VMEM((rows, WIDTH), jnp.bfloat16),
                pltpu.VMEM((rows, WIDTH), jnp.bfloat16),
                pltpu.VMEM((tiles, HEADS * ROWS, TILE), jnp.bfloat16),
                pltpu.VMEM((HEADS, ROWS, TILE), jnp.float32),
                pltpu.VMEM((8, TILE), jnp.float32),
                pltpu.SMEM((tiles,), jnp.int32),
                pltpu.SemaphoreType.DMA((4,)),
            ],
        ),
        compiler_params=pltpu.CompilerParams(vmem_limit_bytes=VMEM_LIMIT),
        cost_estimate=pl.CostEstimate(flops=6 * 10**9, bytes_accessed=18 * 10**6, transcendentals=12 * 10**6),
    )(blk, flags, queries, context_keys, span_keys, context_values, span_values)


SHIFTS = ((0, 0), (1, 0), (0, 1), (0, 3), (1, 1), (1, 3), (0, 2), (1, 2))


def spread_kernel(
    zs, nq_ref, nk_ref, nv_ref, q_ref, k_ref, v_ref, stage,
    keep_sem, q_send, q_recv, kv_send, kv_recv, own_send, ring_recv, pass_send, far_recv, sib_send, sib_recv,
):
    blk = lax.axis_index("blk")
    uly = lax.axis_index("uly")
    ulys = lax.axis_size("uly")
    z, core = blk // 2, blk % 2
    sibling = {"blk": z * 2 + 1 - core}
    ahead = {"blk": lax.rem(z + 1, zs) * 2 + core}
    behind = {"blk": lax.rem(z + zs - 1, zs) * 2 + core}
    height = nq_ref.shape[0]

    barrier = pltpu.get_barrier_semaphore()
    for d in range(1, ulys):
        pl.semaphore_signal(barrier, inc=1, device_id={"uly": lax.rem(uly + d, ulys)}, device_id_type=MESH)
    for device in (sibling, ahead, behind):
        pl.semaphore_signal(barrier, inc=1, device_id=device, device_id_type=MESH)

    def columns(u):
        return pl.ds(pl.multiple_of(u * WIDTH, WIDTH), WIDTH)

    def span_rows(u):
        return pl.ds(pl.multiple_of(u * height, height), height)

    def partner(d, sign):
        across, along = SHIFTS[d]
        return lax.rem(uly // 4 + across, 2) * 4 + lax.rem(uly + 4 + sign * along, 4)

    def q_rows(chip, side, d):
        source = partner(d, -1)
        return pl.ds(pl.multiple_of(((chip * 2 + side) * ulys + source) * height, height), height)

    def q_copy(d):
        target = partner(d, 1)
        return pltpu.make_async_remote_copy(
            src_ref=nq_ref.at[:, columns(target)], dst_ref=q_ref.at[q_rows(z, core, 0), :],
            send_sem=q_send.at[d], recv_sem=q_recv.at[d], device_id={"uly": target}, device_id_type=MESH,
        )

    def kv_copy(which, d):
        target = partner(d, 1)
        src, dst = ((nk_ref, k_ref), (nv_ref, v_ref))[which]
        return pltpu.make_async_remote_copy(
            src_ref=src.at[:, columns(target)], dst_ref=dst.at[span_rows(uly), :],
            send_sem=kv_send.at[which, d], recv_sem=kv_recv.at[which, d],
            device_id={"uly": target}, device_id_type=MESH,
        )

    def kv_wait(which, d):
        src, dst = ((nk_ref, k_ref), (nv_ref, v_ref))[which]
        return pltpu.make_async_remote_copy(
            src_ref=src.at[:, columns(uly)], dst_ref=dst.at[span_rows(partner(d, -1)), :],
            send_sem=kv_send.at[which, d], recv_sem=kv_recv.at[which, d],
            device_id={"uly": partner(d, 1)}, device_id_type=MESH,
        )

    def move(rows, send, recv, device):
        return pltpu.make_async_remote_copy(
            src_ref=q_ref.at[rows, :], dst_ref=q_ref.at[rows, :],
            send_sem=send, recv_sem=recv, device_id=device, device_id_type=MESH,
        )

    chips = [z, lax.rem(z + zs - 1, zs), lax.rem(z + 1, zs), lax.rem(z + 2, zs)]

    def to_sibling(slot, d):
        return move(q_rows(chips[slot], core, d), sib_send.at[slot, d], sib_recv.at[slot, d], sibling)

    def from_sibling(slot, d):
        return move(q_rows(chips[slot], 1 - core, d), sib_send.at[slot, d], sib_recv.at[slot, d], sibling)

    def to_ring(way, d):
        return move(q_rows(z, core, d), own_send.at[way, d], ring_recv.at[way, d], (ahead, behind)[way])

    def from_ring(way, d):
        return move(q_rows(chips[1 + way], core, d), own_send.at[way, d], ring_recv.at[way, d], (ahead, behind)[way])

    def onward(way, d):
        return move(q_rows(chips[1 + way], core, d), pass_send.at[d], far_recv.at[d], (ahead, behind)[way])

    def from_far(d):
        return move(q_rows(chips[3], core, d), pass_send.at[d], far_recv.at[d], (ahead, behind)[d % 2])

    fetches = [
        pltpu.make_async_copy(src.at[:, columns(uly)], stage.at[i], keep_sem.at[i])
        for i, src in enumerate((nq_ref, nk_ref, nv_ref))
    ]
    keeps = [
        pltpu.make_async_copy(stage.at[i], dst, keep_sem.at[i])
        for i, dst in enumerate(
            (q_ref.at[q_rows(z, core, 0), :], k_ref.at[span_rows(uly), :], v_ref.at[span_rows(uly), :])
        )
    ]
    for fetch in fetches:
        fetch.start()
    for fetch in fetches:
        fetch.wait()
    pl.semaphore_wait(barrier, ulys - 1 + 3)

    def own_piece(send, recv, device):
        return pltpu.make_async_remote_copy(
            src_ref=stage.at[0], dst_ref=q_ref.at[q_rows(z, core, 0), :],
            send_sem=send, recv_sem=recv, device_id=device, device_id_type=MESH,
        )

    own_piece(own_send.at[0, 0], ring_recv.at[0, 0], ahead).start()
    own_piece(own_send.at[1, 0], ring_recv.at[1, 0], behind).start()
    for d in range(1, 1 + FLIGHT):
        q_copy(d).start()
    own_piece(sib_send.at[0, 0], sib_recv.at[0, 0], sibling).start()
    for keep in keeps:
        keep.start()

    for d in range(1, ulys):
        move(q_rows(z, core, d), q_send.at[d], q_recv.at[d], sibling).wait_recv()
        if d + FLIGHT < ulys:
            q_copy(d).wait_send()
            q_copy(d + FLIGHT).start()
        to_ring(0, d).start()
        to_ring(1, d).start()
        to_sibling(0, d).start()
    for which in range(2):
        for d in range(1, ulys):
            kv_copy(which, d).start()
    for d in range(ulys):
        for way in range(2):
            from_ring(way, d).wait_recv()
            if d % 2 == way:
                onward(way, d).start()
            to_sibling(1 + way, d).start()
    for d in range(ulys):
        from_far(d).wait_recv()
        to_sibling(3, d).start()

    for d in range(1, ulys):
        if d + FLIGHT >= ulys:
            q_copy(d).wait_send()
        for which in range(2):
            kv_copy(which, d).wait_send()
            kv_wait(which, d).wait_recv()
    for keep in keeps:
        keep.wait()
    for d in range(ulys):
        to_ring(0, d).wait_send()
        to_ring(1, d).wait_send()
        onward(d % 2, d).wait_send()
        for slot in range(4):
            to_sibling(slot, d).wait_send()
            from_sibling(slot, d).wait_recv()


def spread(new_queries, new_keys, new_values, zs, ulys):
    height = new_queries.shape[0]
    dma = pltpu.SemaphoreType.DMA
    anywhere = pl.BlockSpec(memory_space=pl.ANY)
    span = jax.ShapeDtypeStruct((height * ulys, WIDTH), jnp.bfloat16)
    return pl.pallas_call(
        functools.partial(spread_kernel, zs),
        out_shape=(jax.ShapeDtypeStruct((height * ulys * zs * 2, WIDTH), jnp.bfloat16), span, span),
        in_specs=[pl.BlockSpec(memory_space=pltpu.HBM)] * 3,
        out_specs=(anywhere,) * 3,
        scratch_shapes=[
            pltpu.VMEM((3, height, WIDTH), jnp.bfloat16),
            dma((3,)), dma((ulys,)), dma((ulys,)),
            dma((2, ulys)), dma((2, ulys)),
            dma((2, ulys)), dma((2, ulys)),
            dma((ulys,)), dma((ulys,)),
            dma((4, ulys)), dma((4, ulys)),
        ],
        compiler_params=pltpu.CompilerParams(
            collective_id=0, has_side_effects=True, vmem_limit_bytes=VMEM_LIMIT
        ),
        cost_estimate=pl.CostEstimate(flops=0, bytes_accessed=2 * 10**7, transcendentals=0),
    )(new_queries, new_keys, new_values)


def merge(pieces):
    logs = []
    for ref, at in pieces:
        both = ref[at, WIDTH:PIECE, :].astype(jnp.float32)
        logs.append(both[:8] + both[8:])
    best = functools.reduce(jnp.maximum, logs)
    weights = [jnp.exp2(log - best) for log in logs]
    total = functools.reduce(jnp.add, weights)
    inverse = 1.0 / total
    shares = [w * inverse for w in weights]
    return shares, best + jnp.log2(total)


def head_sum(pieces, shares, h):
    found = None
    for (ref, at), share in zip(pieces, shares):
        term = ref[at, h * DH : (h + 1) * DH, :].astype(jnp.float32) * share[h : h + 1, :]
        found = term if found is None else found + term
    return found


def join_kernel(
    zs, part_ref, out_ref, own, sib, far, near, send_far, send_near, done,
    own_sem, sib_send, sib_recv, far_send, far_recv, near_send, near_recv, out_send, out_recv, out_local,
):
    blk = lax.axis_index("blk")
    uly = lax.axis_index("uly")
    z, core = blk // 2, blk % 2
    ring = [lax.rem(z + d, zs) for d in (2, 1, zs - 1, 0)]
    sibling = {"blk": z * 2 + 1 - core}
    ahead = {"blk": ring[1] * 2 + core}
    behind = {"blk": ring[2] * 2 + core}
    ulys = lax.axis_size("uly")
    tiles = own.shape[1]

    barrier = pltpu.get_barrier_semaphore()
    for device in (sibling, ahead, behind):
        pl.semaphore_signal(barrier, inc=1, device_id=device, device_id_type=MESH)
    for d in range(1, ulys):
        pl.semaphore_signal(barrier, inc=1, device_id={"uly": lax.rem(uly + d, ulys)}, device_id_type=MESH)

    def turned(t):
        return lax.rem(t + uly, tiles)

    def own_copy(slot, t):
        index = (ring[slot] * 2 + core) * tiles + turned(t)
        return pltpu.make_async_copy(part_ref.at[index], own.at[slot, t], own_sem.at[slot, t])

    def sib_copy(slot, t):
        index = (ring[slot] * 2 + 1 - core) * tiles + turned(t)
        return pltpu.make_async_remote_copy(
            src_ref=part_ref.at[index], dst_ref=sib.at[slot, t],
            send_sem=sib_send.at[slot, t], recv_sem=sib_recv.at[slot, t],
            device_id=sibling, device_id_type=MESH,
        )

    def far_copy(t):
        return pltpu.make_async_remote_copy(
            src_ref=send_far.at[t], dst_ref=far.at[t],
            send_sem=far_send.at[t], recv_sem=far_recv.at[t],
            device_id=ahead if t < 2 else behind, device_id_type=MESH,
        )

    def near_copy(way, t):
        return pltpu.make_async_remote_copy(
            src_ref=send_near.at[way, t], dst_ref=near.at[way, t],
            send_sem=near_send.at[way, t], recv_sem=near_recv.at[way, t],
            device_id=ahead if way == 0 else behind, device_id_type=MESH,
        )

    order = [(0, 0), (0, 2), (0, 1), (0, 3)]
    order += [(slot, t) for t in (0, 2, 1, 3) for slot in (1, 2)]
    order += [(3, t) for t in (0, 2, 1, 3)]
    for slot, t in order:
        own_copy(slot, t).start()
    pl.semaphore_wait(barrier, 3 + ulys - 1)
    for slot, t in order:
        sib_copy(slot, t).start()

    def ready(slot, t):
        own_copy(slot, t).wait()
        sib_copy(slot, t).wait_recv()
        return [(own.at[slot], t), (sib.at[slot], t)]

    def store(pieces, dst):
        shares, log = merge(pieces)
        for h in range(HEADS):
            dst[h * DH : (h + 1) * DH, :] = head_sum(pieces, shares, h).astype(jnp.bfloat16)
        dst[WIDTH:PIECE, :] = split_low(log)

    for t in (0, 2, 1, 3):
        store(ready(0, t), send_far.at[t])
        far_copy(t).start()
    for t in (0, 2, 1, 3):
        passed = t // 2
        for way in (1 - passed, passed):
            pieces = ready(way + 1, t)
            if way == passed:
                far_copy(t).wait_recv()
                pieces = pieces + [(far, t)]
            place = (0, 2, 1, 3).index(t)
            store(pieces, send_near.at[way, t])
            if place >= DEPTH:
                near_copy(way, (0, 2, 1, 3)[place - DEPTH]).wait_send()
            near_copy(way, t).start()

    half = out_ref.shape[0]

    def out_copy(i, u):
        return pltpu.make_async_remote_copy(
            src_ref=done.at[i], dst_ref=out_ref.at[:, pl.ds(pl.multiple_of(uly * WIDTH, WIDTH), WIDTH)],
            send_sem=out_send.at[i], recv_sem=out_recv.at[uly],
            device_id={"uly": u}, device_id_type=MESH,
        )

    def out_keep(i):
        return pltpu.make_async_copy(
            done.at[i], out_ref.at[:, pl.ds(pl.multiple_of(uly * WIDTH, WIDTH), WIDTH)], out_local
        )

    for t in (0, 2, 1, 3):
        pieces = ready(3, t)
        near_copy(0, t).wait_recv()
        near_copy(1, t).wait_recv()
        pieces = pieces + [(near.at[0], t), (near.at[1], t)]
        shares, log = merge(pieces)
        for h in range(HEADS):
            flat = head_sum(pieces, shares, h).astype(jnp.bfloat16).T
            for j in range(2):
                done[2 * t + j, :, h * DH : (h + 1) * DH] = flat[j * half : (j + 1) * half]
        for j in range(2):
            u = 2 * turned(t) + j

            @pl.when(uly != u)
            def _():
                out_copy(2 * t + j, u).start()

            @pl.when(uly == u)
            def _():
                out_keep(2 * t + j).start()

    out_keep(0).wait()
    for i in range(ulys):
        u = 2 * turned(i // 2) + i % 2

        @pl.when(uly != u)
        def _():
            out_copy(i, u).wait_send()
            pltpu.make_async_remote_copy(
                src_ref=done.at[i], dst_ref=out_ref.at[:, pl.ds(pl.multiple_of(u * WIDTH, WIDTH), WIDTH)],
                send_sem=out_send.at[i], recv_sem=out_recv.at[u],
                device_id={"uly": u}, device_id_type=MESH,
            ).wait_recv()

    for slot, t in order:
        sib_copy(slot, t).wait_send()
    for t in range(tiles):
        far_copy(t).wait_send()
        if (0, 2, 1, 3).index(t) >= tiles - DEPTH:
            near_copy(0, t).wait_send()
            near_copy(1, t).wait_send()


def join(part, rows, zs, ulys):
    tiles = part.shape[0] // (2 * zs)
    piece = (PIECE, TILE)
    dma = pltpu.SemaphoreType.DMA
    return pl.pallas_call(
        functools.partial(join_kernel, zs),
        out_shape=jax.ShapeDtypeStruct((rows, ulys * WIDTH), jnp.bfloat16),
        in_specs=[pl.BlockSpec(memory_space=pl.ANY)],
        out_specs=pl.BlockSpec(memory_space=pl.ANY),
        scratch_shapes=[
            pltpu.VMEM((4, tiles) + piece, jnp.bfloat16),
            pltpu.VMEM((4, tiles) + piece, jnp.bfloat16),
            pltpu.VMEM((tiles,) + piece, jnp.bfloat16),
            pltpu.VMEM((2, tiles) + piece, jnp.bfloat16),
            pltpu.VMEM((tiles,) + piece, jnp.bfloat16),
            pltpu.VMEM((2, tiles) + piece, jnp.bfloat16),
            pltpu.VMEM((ulys, rows, WIDTH), jnp.bfloat16),
            dma((4, tiles)), dma((4, tiles)), dma((4, tiles)),
            dma((tiles,)), dma((tiles,)),
            dma((2, tiles)), dma((2, tiles)),
            dma((ulys,)), dma((ulys,)), dma,
        ],
        compiler_params=pltpu.CompilerParams(
            collective_id=1, has_side_effects=True, vmem_limit_bytes=48 * 1024 * 1024
        ),
        cost_estimate=pl.CostEstimate(flops=2 * 10**7, bytes_accessed=10**7, transcendentals=10**5),
    )(part)


def shards(new_queries, new_keys, new_values, context_keys, context_values, keep_flags):
    zs, ulys = lax.axis_size("blk") // 2, lax.axis_size("uly")
    queries, span_keys, span_values = spread(new_queries, new_keys, new_values, zs, ulys)
    blk = jnp.reshape(lax.axis_index("blk").astype(jnp.int32), (1,))
    part = attend(blk, keep_flags, queries, context_keys, span_keys, context_values, span_values)
    return join(part, new_queries.shape[0], zs, ulys)


def solution(mesh):
    in_specs = (
        P(("cfg", "blk", "uly"), None),
        P(("cfg", "blk", "uly"), None),
        P(("cfg", "blk", "uly"), None),
        P(("cfg", "blk"), "uly"),
        P(("cfg", "blk"), "uly"),
        P(),
    )
    out_specs = P(("cfg", "blk", "uly"), None)
    return jax.shard_map(shards, mesh=mesh, in_specs=in_specs, out_specs=out_specs, check_vma=False)
```

```python
import functools

import jax
import jax.numpy as jnp
from jax import lax
from jax.experimental import pallas as pl
from jax.experimental.pallas import tpu as pltpu
from jax.sharding import PartitionSpec as P

DH = 128
TILE = 128
HEADS = 6
WIDTH = HEADS * DH
ROWS = 144
PIECE = WIDTH + 16
GROUP = 6
STRIDE = 16
LAG = 6
VMEM_LIMIT = 62 * 1024 * 1024
FLIGHT = 7
DEPTH = 1
LOW = -1e30
LOG2 = 1.4426950408889634 * DH ** (-0.5)
MESH = pl.DeviceIdType.MESH


def split_low(x):
    high = x.astype(jnp.bfloat16).astype(jnp.float32)
    return jnp.concatenate([high, x - high], axis=0).astype(jnp.bfloat16)


def attend_kernel(
    blk_ref, flags_ref, q_ref, ck_ref, sk_ref, cv_ref, sv_ref, o_ref,
    k_ref, v_ref, vt, acc, top, q_buf, o_buf, k_list, counts, ranked, places, sems, q_sems, o_sems,
):
    q_tiles = o_ref.shape[0]
    empty = vt.shape[0] - 1
    tiles = empty
    ctx_rows = ck_ref.shape[0]
    ctx_tiles = ctx_rows // TILE
    span_tiles = tiles - ctx_tiles
    blk = blk_ref[0]
    first_span = flags_ref.shape[1] - flags_ref.shape[0]
    pairs = q_tiles // 2

    copies = [
        pltpu.make_async_copy(cv_ref, v_ref.at[:ctx_rows], sems.at[0]),
        pltpu.make_async_copy(sv_ref, v_ref.at[ctx_rows:], sems.at[1]),
        pltpu.make_async_copy(ck_ref, k_ref.at[:ctx_rows], sems.at[2]),
        pltpu.make_async_copy(sk_ref, k_ref.at[ctx_rows:], sems.at[3]),
    ]
    for copy in copies:
        copy.start()

    for c in range(tiles + 1):
        places[c] = 0

    def gather(step, carry):
        near = [2 * step, 2 * step + 1]
        flags = [
            [flags_ref[tile, blk * ctx_tiles + t] for t in range(ctx_tiles)]
            + [flags_ref[tile, first_span + blk * span_tiles + t] for t in range(span_tiles)]
            for tile in near
        ]
        for tile, row in zip(near, flags):
            base = tile * STRIDE
            count = jnp.int32(0)
            for t in range(tiles):
                k_list[base + count] = t
                count = count + row[t]
            counts[tile] = count
            places[count] = places[count] + 1
        return carry

    lax.fori_loop(0, pairs, gather, 0)
    run = jnp.int32(0)
    for c in range(tiles, -1, -1):
        held = places[c]
        places[c] = run
        run = run + held

    def rank(tile, carry):
        count = counts[tile]
        place = places[count]
        ranked[place] = tile
        places[count] = place + 1
        return carry

    lax.fori_loop(0, q_tiles, rank, 0)

    def q_copy(pair, slot, i):
        tile = ranked[2 * pair + i]
        rows = pl.ds(pl.multiple_of(tile * TILE, TILE), TILE)
        return pltpu.make_async_copy(q_ref.at[rows, :], q_buf.at[slot, i], q_sems.at[slot, i])

    def o_copy(tile, slot, i):
        return pltpu.make_async_copy(o_buf.at[slot, i], o_ref.at[tile], o_sems.at[slot, i])

    for i in range(2):
        q_copy(0, 0, i).start()
    copies[0].wait()
    copies[1].wait()

    def turn(t, carry):
        rows = pl.ds(pl.multiple_of(t * TILE, TILE), TILE)
        for h in range(HEADS):
            vt[t, h * ROWS : h * ROWS + DH, :] = v_ref[rows, h * DH : (h + 1) * DH].T
            vt[t, h * ROWS + DH : (h + 1) * ROWS, :] = jnp.ones((ROWS - DH, TILE), jnp.bfloat16)
        return carry

    lax.fori_loop(0, tiles, turn, 0)
    vt[empty] = jnp.zeros(vt.shape[1:], vt.dtype)
    top[...] = jnp.full_like(top, LOW)
    copies[2].wait()
    copies[3].wait()

    def one(pair, carry):
        slot = lax.rem(pair, 2)

        @pl.when(pair + 1 < pairs)
        def _():
            for i in range(2):
                q_copy(pair + 1, 1 - slot, i).start()

        both = [ranked[2 * pair], ranked[2 * pair + 1]]
        kept = [counts[tile] for tile in both]
        n = jnp.maximum(kept[0], 1)
        for i in range(2):
            q_copy(pair, slot, i).wait()

        def scores(i, h, ks):
            cols = slice(h * DH, (h + 1) * DH)
            return lax.dot_general(
                jnp.concatenate([k_ref[pl.ds(pl.multiple_of(t * TILE, TILE), TILE), cols] for t in ks], axis=0),
                q_buf[slot, i, :, cols],
                (((1,), (1,)), ((), ())),
                preferred_element_type=jnp.float32,
            )

        def weigh(i, h, vs, s, first):
            new = jnp.max(s, axis=0, keepdims=True)
            if not first:
                old = top[i, h : h + 1, :]
                new = jnp.maximum(old, new)
                scale = jnp.exp2((old - new) * LOG2)
            top[i, h : h + 1, :] = new
            p = jnp.exp2((s - new) * LOG2).astype(jnp.bfloat16)
            values = jnp.concatenate([vt[t, h * ROWS : (h + 1) * ROWS, :] for t in vs], axis=1)
            got = jnp.dot(values, p, preferred_element_type=jnp.float32)
            acc[i, h] = got if first else acc[i, h] * scale + got

        def visit(at, width, first):
            ks = [
                [k_list[tile * STRIDE + jnp.minimum(at + a, jnp.maximum(count - 1, 0))] for a in range(width)]
                for tile, count in zip(both, kept)
            ]
            vs = [
                [jnp.where(at + a < count, ks[i][a], empty) for a in range(width)] for i, count in enumerate(kept)
            ]
            work = [(i, h) for i in range(2) for h in range(HEADS)]
            found = [scores(i, h, ks[i]) for i, h in work[:LAG]]
            for j, (i, h) in enumerate(work):
                if j + LAG < len(work):
                    i2, h2 = work[j + LAG]
                    found.append(scores(i2, h2, ks[i2]))
                weigh(i, h, vs[i], found[j], first)

        lead = lax.rem(n + GROUP - 1, GROUP) + 1
        lax.switch(lead - 1, [functools.partial(visit, 0, w, True) for w in range(1, GROUP + 1)])

        def more(j, inner):
            visit(lead + GROUP * j, GROUP, False)
            return inner

        lax.fori_loop(0, (n - lead) // GROUP, more, 0)

        @pl.when(pair >= 2)
        def _():
            for i in range(2):
                o_copy(0, slot, i).wait()

        for i in range(2):
            totals = [acc[i, h, DH : DH + 1, :] for h in range(HEADS)]
            for h in range(HEADS):
                safe = jnp.where(totals[h] > 0, totals[h], 1.0)
                o_buf[slot, i, h * DH : (h + 1) * DH, :] = (acc[i, h, :DH, :] * (1.0 / safe)).astype(jnp.bfloat16)
            total = jnp.concatenate(totals + [jnp.zeros((8 - HEADS, TILE), jnp.float32)], axis=0)
            seen = total > 0
            lse = jnp.where(seen, top[i] * LOG2 + jnp.log2(jnp.where(seen, total, 1.0)), LOW)
            o_buf[slot, i, WIDTH:PIECE, :] = split_low(lse)
            o_copy(both[i], slot, i).start()
        return carry

    lax.fori_loop(0, pairs, one, 0)
    for slot in range(2):
        for i in range(2):
            o_copy(0, slot, i).wait()


def attend(blk, flags, queries, context_keys, span_keys, context_values, span_values):
    steps = queries.shape[0] // TILE
    rows = context_keys.shape[0] + span_keys.shape[0]
    tiles = rows // TILE
    anywhere = pl.BlockSpec(memory_space=pl.ANY)
    number = pltpu.SMEM
    return pl.pallas_call(
        attend_kernel,
        out_shape=jax.ShapeDtypeStruct((steps, PIECE, TILE), jnp.bfloat16),
        grid_spec=pltpu.PrefetchScalarGridSpec(
            num_scalar_prefetch=2,
            grid=(1,),
            in_specs=[anywhere] * 5,
            out_specs=anywhere,
            scratch_shapes=[
                pltpu.VMEM((rows, WIDTH), jnp.bfloat16),
                pltpu.VMEM((rows, WIDTH), jnp.bfloat16),
                pltpu.VMEM((tiles + 1, HEADS * ROWS, TILE), jnp.bfloat16),
                pltpu.VMEM((2, HEADS, ROWS, TILE), jnp.float32),
                pltpu.VMEM((2, 8, TILE), jnp.float32),
                pltpu.VMEM((2, 2, TILE, WIDTH), jnp.bfloat16),
                pltpu.VMEM((2, 2, PIECE, TILE), jnp.bfloat16),
                number((steps * STRIDE,), jnp.int32),
                number((steps,), jnp.int32),
                number((steps,), jnp.int32),
                number((tiles + 1,), jnp.int32),
                pltpu.SemaphoreType.DMA((4,)),
                pltpu.SemaphoreType.DMA((2, 2)),
                pltpu.SemaphoreType.DMA((2, 2)),
            ],
        ),
        compiler_params=pltpu.CompilerParams(vmem_limit_bytes=VMEM_LIMIT),
        cost_estimate=pl.CostEstimate(flops=6 * 10**9, bytes_accessed=18 * 10**6, transcendentals=12 * 10**6),
    )(blk, flags, queries, context_keys, span_keys, context_values, span_values)


SHIFTS = ((0, 0), (1, 0), (0, 1), (0, 3), (1, 1), (1, 3), (0, 2), (1, 2))


def spread_kernel(
    zs, nq_ref, nk_ref, nv_ref, q_ref, k_ref, v_ref, stage,
    keep_sem, q_send, q_recv, kv_send, kv_recv, own_send, ring_recv, pass_send, far_recv, sib_send, sib_recv,
):
    blk = lax.axis_index("blk")
    uly = lax.axis_index("uly")
    ulys = lax.axis_size("uly")
    z, core = blk // 2, blk % 2
    sibling = {"blk": z * 2 + 1 - core}
    ahead = {"blk": lax.rem(z + 1, zs) * 2 + core}
    behind = {"blk": lax.rem(z + zs - 1, zs) * 2 + core}
    height = nq_ref.shape[0]

    barrier = pltpu.get_barrier_semaphore()
    for d in range(1, ulys):
        pl.semaphore_signal(barrier, inc=1, device_id={"uly": lax.rem(uly + d, ulys)}, device_id_type=MESH)
    for device in (sibling, ahead, behind):
        pl.semaphore_signal(barrier, inc=1, device_id=device, device_id_type=MESH)

    def columns(u):
        return pl.ds(pl.multiple_of(u * WIDTH, WIDTH), WIDTH)

    def span_rows(u):
        return pl.ds(pl.multiple_of(u * height, height), height)

    def partner(d, sign):
        across, along = SHIFTS[d]
        return lax.rem(uly // 4 + across, 2) * 4 + lax.rem(uly + 4 + sign * along, 4)

    def q_rows(chip, side, d):
        source = partner(d, -1)
        return pl.ds(pl.multiple_of(((chip * 2 + side) * ulys + source) * height, height), height)

    def q_copy(d):
        target = partner(d, 1)
        return pltpu.make_async_remote_copy(
            src_ref=nq_ref.at[:, columns(target)], dst_ref=q_ref.at[q_rows(z, core, 0), :],
            send_sem=q_send.at[d], recv_sem=q_recv.at[d], device_id={"uly": target}, device_id_type=MESH,
        )

    def kv_copy(which, d):
        target = partner(d, 1)
        src, dst = ((nk_ref, k_ref), (nv_ref, v_ref))[which]
        return pltpu.make_async_remote_copy(
            src_ref=src.at[:, columns(target)], dst_ref=dst.at[span_rows(uly), :],
            send_sem=kv_send.at[which, d], recv_sem=kv_recv.at[which, d],
            device_id={"uly": target}, device_id_type=MESH,
        )

    def kv_wait(which, d):
        src, dst = ((nk_ref, k_ref), (nv_ref, v_ref))[which]
        return pltpu.make_async_remote_copy(
            src_ref=src.at[:, columns(uly)], dst_ref=dst.at[span_rows(partner(d, -1)), :],
            send_sem=kv_send.at[which, d], recv_sem=kv_recv.at[which, d],
            device_id={"uly": partner(d, 1)}, device_id_type=MESH,
        )

    def move(rows, send, recv, device):
        return pltpu.make_async_remote_copy(
            src_ref=q_ref.at[rows, :], dst_ref=q_ref.at[rows, :],
            send_sem=send, recv_sem=recv, device_id=device, device_id_type=MESH,
        )

    chips = [z, lax.rem(z + zs - 1, zs), lax.rem(z + 1, zs), lax.rem(z + 2, zs)]

    def to_sibling(slot, d):
        return move(q_rows(chips[slot], core, d), sib_send.at[slot, d], sib_recv.at[slot, d], sibling)

    def from_sibling(slot, d):
        return move(q_rows(chips[slot], 1 - core, d), sib_send.at[slot, d], sib_recv.at[slot, d], sibling)

    def to_ring(way, d):
        return move(q_rows(z, core, d), own_send.at[way, d], ring_recv.at[way, d], (ahead, behind)[way])

    def from_ring(way, d):
        return move(q_rows(chips[1 + way], core, d), own_send.at[way, d], ring_recv.at[way, d], (ahead, behind)[way])

    def onward(way, d):
        return move(q_rows(chips[1 + way], core, d), pass_send.at[d], far_recv.at[d], (ahead, behind)[way])

    def from_far(d):
        return move(q_rows(chips[3], core, d), pass_send.at[d], far_recv.at[d], (ahead, behind)[d % 2])

    fetches = [
        pltpu.make_async_copy(src.at[:, columns(uly)], stage.at[i], keep_sem.at[i])
        for i, src in enumerate((nq_ref, nk_ref, nv_ref))
    ]
    keeps = [
        pltpu.make_async_copy(stage.at[i], dst, keep_sem.at[i])
        for i, dst in enumerate(
            (q_ref.at[q_rows(z, core, 0), :], k_ref.at[span_rows(uly), :], v_ref.at[span_rows(uly), :])
        )
    ]
    for fetch in fetches:
        fetch.start()
    for fetch in fetches:
        fetch.wait()
    pl.semaphore_wait(barrier, ulys - 1 + 3)

    def own_piece(send, recv, device):
        return pltpu.make_async_remote_copy(
            src_ref=stage.at[0], dst_ref=q_ref.at[q_rows(z, core, 0), :],
            send_sem=send, recv_sem=recv, device_id=device, device_id_type=MESH,
        )

    own_piece(own_send.at[0, 0], ring_recv.at[0, 0], ahead).start()
    own_piece(own_send.at[1, 0], ring_recv.at[1, 0], behind).start()
    for d in range(1, 1 + FLIGHT):
        q_copy(d).start()
    own_piece(sib_send.at[0, 0], sib_recv.at[0, 0], sibling).start()
    for keep in keeps:
        keep.start()

    for d in range(1, ulys):
        move(q_rows(z, core, d), q_send.at[d], q_recv.at[d], sibling).wait_recv()
        if d + FLIGHT < ulys:
            q_copy(d).wait_send()
            q_copy(d + FLIGHT).start()
        to_ring(0, d).start()
        to_ring(1, d).start()
        to_sibling(0, d).start()
    for which in range(2):
        for d in range(1, ulys):
            kv_copy(which, d).start()
    for d in range(ulys):
        for way in range(2):
            from_ring(way, d).wait_recv()
            if d % 2 == way:
                onward(way, d).start()
            to_sibling(1 + way, d).start()
    for d in range(ulys):
        from_far(d).wait_recv()
        to_sibling(3, d).start()

    for d in range(1, ulys):
        if d + FLIGHT >= ulys:
            q_copy(d).wait_send()
        for which in range(2):
            kv_copy(which, d).wait_send()
            kv_wait(which, d).wait_recv()
    for keep in keeps:
        keep.wait()
    for d in range(ulys):
        to_ring(0, d).wait_send()
        to_ring(1, d).wait_send()
        onward(d % 2, d).wait_send()
        for slot in range(4):
            to_sibling(slot, d).wait_send()
            from_sibling(slot, d).wait_recv()


def spread(new_queries, new_keys, new_values, zs, ulys):
    height = new_queries.shape[0]
    dma = pltpu.SemaphoreType.DMA
    anywhere = pl.BlockSpec(memory_space=pl.ANY)
    span = jax.ShapeDtypeStruct((height * ulys, WIDTH), jnp.bfloat16)
    return pl.pallas_call(
        functools.partial(spread_kernel, zs),
        out_shape=(jax.ShapeDtypeStruct((height * ulys * zs * 2, WIDTH), jnp.bfloat16), span, span),
        in_specs=[pl.BlockSpec(memory_space=pltpu.HBM)] * 3,
        out_specs=(anywhere,) * 3,
        scratch_shapes=[
            pltpu.VMEM((3, height, WIDTH), jnp.bfloat16),
            dma((3,)), dma((ulys,)), dma((ulys,)),
            dma((2, ulys)), dma((2, ulys)),
            dma((2, ulys)), dma((2, ulys)),
            dma((ulys,)), dma((ulys,)),
            dma((4, ulys)), dma((4, ulys)),
        ],
        compiler_params=pltpu.CompilerParams(
            collective_id=0, has_side_effects=True, vmem_limit_bytes=VMEM_LIMIT
        ),
        cost_estimate=pl.CostEstimate(flops=0, bytes_accessed=2 * 10**7, transcendentals=0),
    )(new_queries, new_keys, new_values)


def merge(pieces):
    logs = []
    for ref, at in pieces:
        both = ref[at, WIDTH:PIECE, :].astype(jnp.float32)
        logs.append(both[:8] + both[8:])
    best = functools.reduce(jnp.maximum, logs)
    weights = [jnp.exp2(log - best) for log in logs]
    total = functools.reduce(jnp.add, weights)
    inverse = 1.0 / total
    shares = [w * inverse for w in weights]
    return shares, best + jnp.log2(total)


def head_sum(pieces, shares, h):
    found = None
    for (ref, at), share in zip(pieces, shares):
        term = ref[at, h * DH : (h + 1) * DH, :].astype(jnp.float32) * share[h : h + 1, :]
        found = term if found is None else found + term
    return found


def join_kernel(
    zs, part_ref, out_ref, own, sib, far, near, send_far, send_near, done,
    own_sem, sib_send, sib_recv, far_send, far_recv, near_send, near_recv, out_send, out_recv, out_local,
):
    blk = lax.axis_index("blk")
    uly = lax.axis_index("uly")
    z, core = blk // 2, blk % 2
    ring = [lax.rem(z + d, zs) for d in (2, 1, zs - 1, 0)]
    sibling = {"blk": z * 2 + 1 - core}
    ahead = {"blk": ring[1] * 2 + core}
    behind = {"blk": ring[2] * 2 + core}
    ulys = lax.axis_size("uly")
    tiles = own.shape[1]

    barrier = pltpu.get_barrier_semaphore()
    for device in (sibling, ahead, behind):
        pl.semaphore_signal(barrier, inc=1, device_id=device, device_id_type=MESH)
    for d in range(1, ulys):
        pl.semaphore_signal(barrier, inc=1, device_id={"uly": lax.rem(uly + d, ulys)}, device_id_type=MESH)

    def turned(t):
        return lax.rem(t + uly, tiles)

    def own_copy(slot, t):
        index = (ring[slot] * 2 + core) * tiles + turned(t)
        return pltpu.make_async_copy(part_ref.at[index], own.at[slot, t], own_sem.at[slot, t])

    def sib_copy(slot, t):
        index = (ring[slot] * 2 + 1 - core) * tiles + turned(t)
        return pltpu.make_async_remote_copy(
            src_ref=part_ref.at[index], dst_ref=sib.at[slot, t],
            send_sem=sib_send.at[slot, t], recv_sem=sib_recv.at[slot, t],
            device_id=sibling, device_id_type=MESH,
        )

    def far_copy(t):
        return pltpu.make_async_remote_copy(
            src_ref=send_far.at[t], dst_ref=far.at[t],
            send_sem=far_send.at[t], recv_sem=far_recv.at[t],
            device_id=ahead if t < 2 else behind, device_id_type=MESH,
        )

    def near_copy(way, t):
        return pltpu.make_async_remote_copy(
            src_ref=send_near.at[way, t], dst_ref=near.at[way, t],
            send_sem=near_send.at[way, t], recv_sem=near_recv.at[way, t],
            device_id=ahead if way == 0 else behind, device_id_type=MESH,
        )

    order = [(0, 0), (0, 2), (0, 1), (0, 3)]
    order += [(slot, t) for t in (0, 2, 1, 3) for slot in (1, 2)]
    order += [(3, t) for t in (0, 2, 1, 3)]
    for slot, t in order:
        own_copy(slot, t).start()
    pl.semaphore_wait(barrier, 3 + ulys - 1)
    for slot, t in order:
        sib_copy(slot, t).start()

    def ready(slot, t):
        own_copy(slot, t).wait()
        sib_copy(slot, t).wait_recv()
        return [(own.at[slot], t), (sib.at[slot], t)]

    def store(pieces, dst):
        shares, log = merge(pieces)
        for h in range(HEADS):
            dst[h * DH : (h + 1) * DH, :] = head_sum(pieces, shares, h).astype(jnp.bfloat16)
        dst[WIDTH:PIECE, :] = split_low(log)

    for t in (0, 2, 1, 3):
        store(ready(0, t), send_far.at[t])
        far_copy(t).start()
    for t in (0, 2, 1, 3):
        passed = t // 2
        for way in (1 - passed, passed):
            pieces = ready(way + 1, t)
            if way == passed:
                far_copy(t).wait_recv()
                pieces = pieces + [(far, t)]
            place = (0, 2, 1, 3).index(t)
            store(pieces, send_near.at[way, t])
            if place >= DEPTH:
                near_copy(way, (0, 2, 1, 3)[place - DEPTH]).wait_send()
            near_copy(way, t).start()

    half = out_ref.shape[0]

    def out_copy(i, u):
        return pltpu.make_async_remote_copy(
            src_ref=done.at[i], dst_ref=out_ref.at[:, pl.ds(pl.multiple_of(uly * WIDTH, WIDTH), WIDTH)],
            send_sem=out_send.at[i], recv_sem=out_recv.at[uly],
            device_id={"uly": u}, device_id_type=MESH,
        )

    def out_keep(i):
        return pltpu.make_async_copy(
            done.at[i], out_ref.at[:, pl.ds(pl.multiple_of(uly * WIDTH, WIDTH), WIDTH)], out_local
        )

    for t in (0, 2, 1, 3):
        pieces = ready(3, t)
        near_copy(0, t).wait_recv()
        near_copy(1, t).wait_recv()
        pieces = pieces + [(near.at[0], t), (near.at[1], t)]
        shares, log = merge(pieces)
        for h in range(HEADS):
            flat = head_sum(pieces, shares, h).astype(jnp.bfloat16).T
            for j in range(2):
                done[2 * t + j, :, h * DH : (h + 1) * DH] = flat[j * half : (j + 1) * half]
        for j in range(2):
            u = 2 * turned(t) + j

            @pl.when(uly != u)
            def _():
                out_copy(2 * t + j, u).start()

            @pl.when(uly == u)
            def _():
                out_keep(2 * t + j).start()

    out_keep(0).wait()
    for i in range(ulys):
        u = 2 * turned(i // 2) + i % 2

        @pl.when(uly != u)
        def _():
            out_copy(i, u).wait_send()
            pltpu.make_async_remote_copy(
                src_ref=done.at[i], dst_ref=out_ref.at[:, pl.ds(pl.multiple_of(u * WIDTH, WIDTH), WIDTH)],
                send_sem=out_send.at[i], recv_sem=out_recv.at[u],
                device_id={"uly": u}, device_id_type=MESH,
            ).wait_recv()

    for slot, t in order:
        sib_copy(slot, t).wait_send()
    for t in range(tiles):
        far_copy(t).wait_send()
        if (0, 2, 1, 3).index(t) >= tiles - DEPTH:
            near_copy(0, t).wait_send()
            near_copy(1, t).wait_send()


def join(part, rows, zs, ulys):
    tiles = part.shape[0] // (2 * zs)
    piece = (PIECE, TILE)
    dma = pltpu.SemaphoreType.DMA
    return pl.pallas_call(
        functools.partial(join_kernel, zs),
        out_shape=jax.ShapeDtypeStruct((rows, ulys * WIDTH), jnp.bfloat16),
        in_specs=[pl.BlockSpec(memory_space=pl.ANY)],
        out_specs=pl.BlockSpec(memory_space=pl.ANY),
        scratch_shapes=[
            pltpu.VMEM((4, tiles) + piece, jnp.bfloat16),
            pltpu.VMEM((4, tiles) + piece, jnp.bfloat16),
            pltpu.VMEM((tiles,) + piece, jnp.bfloat16),
            pltpu.VMEM((2, tiles) + piece, jnp.bfloat16),
            pltpu.VMEM((tiles,) + piece, jnp.bfloat16),
            pltpu.VMEM((2, tiles) + piece, jnp.bfloat16),
            pltpu.VMEM((ulys, rows, WIDTH), jnp.bfloat16),
            dma((4, tiles)), dma((4, tiles)), dma((4, tiles)),
            dma((tiles,)), dma((tiles,)),
            dma((2, tiles)), dma((2, tiles)),
            dma((ulys,)), dma((ulys,)), dma,
        ],
        compiler_params=pltpu.CompilerParams(
            collective_id=1, has_side_effects=True, vmem_limit_bytes=48 * 1024 * 1024
        ),
        cost_estimate=pl.CostEstimate(flops=2 * 10**7, bytes_accessed=10**7, transcendentals=10**5),
    )(part)


def shards(new_queries, new_keys, new_values, context_keys, context_values, keep_flags):
    zs, ulys = lax.axis_size("blk") // 2, lax.axis_size("uly")
    queries, span_keys, span_values = spread(new_queries, new_keys, new_values, zs, ulys)
    blk = jnp.reshape(lax.axis_index("blk").astype(jnp.int32), (1,))
    part = attend(blk, keep_flags, queries, context_keys, span_keys, context_values, span_values)
    return join(part, new_queries.shape[0], zs, ulys)


def solution(mesh):
    in_specs = (
        P(("cfg", "blk", "uly"), None),
        P(("cfg", "blk", "uly"), None),
        P(("cfg", "blk", "uly"), None),
        P(("cfg", "blk"), "uly"),
        P(("cfg", "blk"), "uly"),
        P(),
    )
    out_specs = P(("cfg", "blk", "uly"), None)
    return jax.shard_map(shards, mesh=mesh, in_specs=in_specs, out_specs=out_specs, check_vma=False)
```

```python
import functools

import jax
import jax.numpy as jnp
from jax import lax
from jax.experimental import pallas as pl
from jax.experimental.pallas import tpu as pltpu
from jax.sharding import PartitionSpec as P

DH = 128
TILE = 128
HEADS = 6
WIDTH = HEADS * DH
ROWS = 144
PIECE = WIDTH + 16
GROUP = 4
STRIDE = 16
LAG = 5
VMEM_LIMIT = 62 * 1024 * 1024
FLIGHT = 7
DEPTH = 1
LOW = -1e30
LOG2 = 1.4426950408889634 * DH ** (-0.5)
MESH = pl.DeviceIdType.MESH


def split_low(x):
    high = x.astype(jnp.bfloat16).astype(jnp.float32)
    return jnp.concatenate([high, x - high], axis=0).astype(jnp.bfloat16)


def attend_kernel(
    blk_ref, flags_ref, q_ref, ck_ref, sk_ref, cv_ref, sv_ref, o_ref,
    k_ref, v_ref, vt, acc, top, q_buf, o_buf, k_list, counts, ranked, places, sems, q_sems, o_sems,
):
    q_tiles = o_ref.shape[0]
    empty = vt.shape[0] - 1
    tiles = empty
    ctx_rows = ck_ref.shape[0]
    ctx_tiles = ctx_rows // TILE
    span_tiles = tiles - ctx_tiles
    blk = blk_ref[0]
    first_span = flags_ref.shape[1] - flags_ref.shape[0]
    pairs = q_tiles // 2

    copies = [
        pltpu.make_async_copy(cv_ref, v_ref.at[:ctx_rows], sems.at[0]),
        pltpu.make_async_copy(sv_ref, v_ref.at[ctx_rows:], sems.at[1]),
        pltpu.make_async_copy(ck_ref, k_ref.at[:ctx_rows], sems.at[2]),
        pltpu.make_async_copy(sk_ref, k_ref.at[ctx_rows:], sems.at[3]),
    ]
    for copy in copies:
        copy.start()

    for c in range(tiles + 1):
        places[c] = 0

    def gather(step, carry):
        near = [2 * step, 2 * step + 1]
        flags = [
            [flags_ref[tile, blk * ctx_tiles + t] for t in range(ctx_tiles)]
            + [flags_ref[tile, first_span + blk * span_tiles + t] for t in range(span_tiles)]
            for tile in near
        ]
        for tile, row in zip(near, flags):
            base = tile * STRIDE
            count = jnp.int32(0)
            for t in range(tiles):
                k_list[base + count] = t
                count = count + row[t]
            counts[tile] = count
            places[count] = places[count] + 1
        return carry

    lax.fori_loop(0, pairs, gather, 0)
    run = jnp.int32(0)
    for c in range(tiles, -1, -1):
        held = places[c]
        places[c] = run
        run = run + held

    def rank(tile, carry):
        count = counts[tile]
        place = places[count]
        ranked[place] = tile
        places[count] = place + 1
        return carry

    lax.fori_loop(0, q_tiles, rank, 0)

    def q_copy(pair, slot, i):
        tile = ranked[2 * pair + i]
        rows = pl.ds(pl.multiple_of(tile * TILE, TILE), TILE)
        return pltpu.make_async_copy(q_ref.at[rows, :], q_buf.at[slot, i], q_sems.at[slot, i])

    def o_copy(tile, slot, i):
        return pltpu.make_async_copy(o_buf.at[slot, i], o_ref.at[tile], o_sems.at[slot, i])

    for i in range(2):
        q_copy(0, 0, i).start()
    copies[0].wait()
    copies[1].wait()

    def turn(t, carry):
        rows = pl.ds(pl.multiple_of(t * TILE, TILE), TILE)
        for h in range(HEADS):
            vt[t, h * ROWS : h * ROWS + DH, :] = v_ref[rows, h * DH : (h + 1) * DH].T
            vt[t, h * ROWS + DH : (h + 1) * ROWS, :] = jnp.ones((ROWS - DH, TILE), jnp.bfloat16)
        return carry

    lax.fori_loop(0, tiles, turn, 0)
    vt[empty] = jnp.zeros(vt.shape[1:], vt.dtype)
    top[...] = jnp.full_like(top, LOW)
    copies[2].wait()
    copies[3].wait()

    def one(pair, carry):
        slot = lax.rem(pair, 2)

        @pl.when(pair + 1 < pairs)
        def _():
            for i in range(2):
                q_copy(pair + 1, 1 - slot, i).start()

        both = [ranked[2 * pair], ranked[2 * pair + 1]]
        kept = [counts[tile] for tile in both]
        n = jnp.maximum(kept[0], 1)
        for i in range(2):
            q_copy(pair, slot, i).wait()

        def scores(i, h, ks):
            cols = slice(h * DH, (h + 1) * DH)
            return lax.dot_general(
                jnp.concatenate([k_ref[pl.ds(pl.multiple_of(t * TILE, TILE), TILE), cols] for t in ks], axis=0),
                q_buf[slot, i, :, cols],
                (((1,), (1,)), ((), ())),
                preferred_element_type=jnp.float32,
            )

        def weigh(i, h, vs, s, first):
            new = jnp.max(s, axis=0, keepdims=True)
            if not first:
                old = top[i, h : h + 1, :]
                new = jnp.maximum(old, new)
                scale = jnp.exp2((old - new) * LOG2)
            top[i, h : h + 1, :] = new
            p = jnp.exp2((s - new) * LOG2).astype(jnp.bfloat16)
            values = jnp.concatenate([vt[t, h * ROWS : (h + 1) * ROWS, :] for t in vs], axis=1)
            got = jnp.dot(values, p, preferred_element_type=jnp.float32)
            acc[i, h] = got if first else acc[i, h] * scale + got

        def visit(at, width, first):
            ks = [
                [k_list[tile * STRIDE + jnp.minimum(at + a, jnp.maximum(count - 1, 0))] for a in range(width)]
                for tile, count in zip(both, kept)
            ]
            vs = [
                [jnp.where(at + a < count, ks[i][a], empty) for a in range(width)] for i, count in enumerate(kept)
            ]
            work = [(i, h) for i in range(2) for h in range(HEADS)]
            found = [scores(i, h, ks[i]) for i, h in work[:LAG]]
            for j, (i, h) in enumerate(work):
                if j + LAG < len(work):
                    i2, h2 = work[j + LAG]
                    found.append(scores(i2, h2, ks[i2]))
                weigh(i, h, vs[i], found[j], first)

        lead = lax.rem(n + GROUP - 1, GROUP) + 1
        lax.switch(lead - 1, [functools.partial(visit, 0, w, True) for w in range(1, GROUP + 1)])

        def more(j, inner):
            visit(lead + GROUP * j, GROUP, False)
            return inner

        lax.fori_loop(0, (n - lead) // GROUP, more, 0)

        @pl.when(pair >= 2)
        def _():
            for i in range(2):
                o_copy(0, slot, i).wait()

        for i in range(2):
            totals = [acc[i, h, DH : DH + 1, :] for h in range(HEADS)]
            for h in range(HEADS):
                safe = jnp.where(totals[h] > 0, totals[h], 1.0)
                o_buf[slot, i, h * DH : (h + 1) * DH, :] = (acc[i, h, :DH, :] * (1.0 / safe)).astype(jnp.bfloat16)
            total = jnp.concatenate(totals + [jnp.zeros((8 - HEADS, TILE), jnp.float32)], axis=0)
            seen = total > 0
            lse = jnp.where(seen, top[i] * LOG2 + jnp.log2(jnp.where(seen, total, 1.0)), LOW)
            o_buf[slot, i, WIDTH:PIECE, :] = split_low(lse)
            o_copy(both[i], slot, i).start()
        return carry

    lax.fori_loop(0, pairs, one, 0)
    for slot in range(2):
        for i in range(2):
            o_copy(0, slot, i).wait()


def attend(blk, flags, queries, context_keys, span_keys, context_values, span_values):
    steps = queries.shape[0] // TILE
    rows = context_keys.shape[0] + span_keys.shape[0]
    tiles = rows // TILE
    anywhere = pl.BlockSpec(memory_space=pl.ANY)
    number = pltpu.SMEM
    return pl.pallas_call(
        attend_kernel,
        out_shape=jax.ShapeDtypeStruct((steps, PIECE, TILE), jnp.bfloat16),
        grid_spec=pltpu.PrefetchScalarGridSpec(
            num_scalar_prefetch=2,
            grid=(1,),
            in_specs=[anywhere] * 5,
            out_specs=anywhere,
            scratch_shapes=[
                pltpu.VMEM((rows, WIDTH), jnp.bfloat16),
                pltpu.VMEM((rows, WIDTH), jnp.bfloat16),
                pltpu.VMEM((tiles + 1, HEADS * ROWS, TILE), jnp.bfloat16),
                pltpu.VMEM((2, HEADS, ROWS, TILE), jnp.float32),
                pltpu.VMEM((2, 8, TILE), jnp.float32),
                pltpu.VMEM((2, 2, TILE, WIDTH), jnp.bfloat16),
                pltpu.VMEM((2, 2, PIECE, TILE), jnp.bfloat16),
                number((steps * STRIDE,), jnp.int32),
                number((steps,), jnp.int32),
                number((steps,), jnp.int32),
                number((tiles + 1,), jnp.int32),
                pltpu.SemaphoreType.DMA((4,)),
                pltpu.SemaphoreType.DMA((2, 2)),
                pltpu.SemaphoreType.DMA((2, 2)),
            ],
        ),
        compiler_params=pltpu.CompilerParams(vmem_limit_bytes=VMEM_LIMIT),
        cost_estimate=pl.CostEstimate(flops=6 * 10**9, bytes_accessed=18 * 10**6, transcendentals=12 * 10**6),
    )(blk, flags, queries, context_keys, span_keys, context_values, span_values)


SHIFTS = ((0, 0), (1, 0), (0, 1), (0, 3), (1, 1), (1, 3), (0, 2), (1, 2))


def spread_kernel(
    zs, nq_ref, nk_ref, nv_ref, q_ref, k_ref, v_ref, stage,
    keep_sem, q_send, q_recv, kv_send, kv_recv, own_send, ring_recv, pass_send, far_recv, sib_send, sib_recv,
):
    blk = lax.axis_index("blk")
    uly = lax.axis_index("uly")
    ulys = lax.axis_size("uly")
    z, core = blk // 2, blk % 2
    sibling = {"blk": z * 2 + 1 - core}
    ahead = {"blk": lax.rem(z + 1, zs) * 2 + core}
    behind = {"blk": lax.rem(z + zs - 1, zs) * 2 + core}
    height = nq_ref.shape[0]

    barrier = pltpu.get_barrier_semaphore()
    for d in range(1, ulys):
        pl.semaphore_signal(barrier, inc=1, device_id={"uly": lax.rem(uly + d, ulys)}, device_id_type=MESH)
    for device in (sibling, ahead, behind):
        pl.semaphore_signal(barrier, inc=1, device_id=device, device_id_type=MESH)

    def columns(u):
        return pl.ds(pl.multiple_of(u * WIDTH, WIDTH), WIDTH)

    def span_rows(u):
        return pl.ds(pl.multiple_of(u * height, height), height)

    def partner(d, sign):
        across, along = SHIFTS[d]
        return lax.rem(uly // 4 + across, 2) * 4 + lax.rem(uly + 4 + sign * along, 4)

    def q_rows(chip, side, d):
        source = partner(d, -1)
        return pl.ds(pl.multiple_of(((chip * 2 + side) * ulys + source) * height, height), height)

    def q_copy(d):
        target = partner(d, 1)
        return pltpu.make_async_remote_copy(
            src_ref=nq_ref.at[:, columns(target)], dst_ref=q_ref.at[q_rows(z, core, 0), :],
            send_sem=q_send.at[d], recv_sem=q_recv.at[d], device_id={"uly": target}, device_id_type=MESH,
        )

    def kv_copy(which, d):
        target = partner(d, 1)
        src, dst = ((nk_ref, k_ref), (nv_ref, v_ref))[which]
        return pltpu.make_async_remote_copy(
            src_ref=src.at[:, columns(target)], dst_ref=dst.at[span_rows(uly), :],
            send_sem=kv_send.at[which, d], recv_sem=kv_recv.at[which, d],
            device_id={"uly": target}, device_id_type=MESH,
        )

    def kv_wait(which, d):
        src, dst = ((nk_ref, k_ref), (nv_ref, v_ref))[which]
        return pltpu.make_async_remote_copy(
            src_ref=src.at[:, columns(uly)], dst_ref=dst.at[span_rows(partner(d, -1)), :],
            send_sem=kv_send.at[which, d], recv_sem=kv_recv.at[which, d],
            device_id={"uly": partner(d, 1)}, device_id_type=MESH,
        )

    def move(rows, send, recv, device):
        return pltpu.make_async_remote_copy(
            src_ref=q_ref.at[rows, :], dst_ref=q_ref.at[rows, :],
            send_sem=send, recv_sem=recv, device_id=device, device_id_type=MESH,
        )

    chips = [z, lax.rem(z + zs - 1, zs), lax.rem(z + 1, zs), lax.rem(z + 2, zs)]

    def to_sibling(slot, d):
        return move(q_rows(chips[slot], core, d), sib_send.at[slot, d], sib_recv.at[slot, d], sibling)

    def from_sibling(slot, d):
        return move(q_rows(chips[slot], 1 - core, d), sib_send.at[slot, d], sib_recv.at[slot, d], sibling)

    def to_ring(way, d):
        return move(q_rows(z, core, d), own_send.at[way, d], ring_recv.at[way, d], (ahead, behind)[way])

    def from_ring(way, d):
        return move(q_rows(chips[1 + way], core, d), own_send.at[way, d], ring_recv.at[way, d], (ahead, behind)[way])

    def onward(way, d):
        return move(q_rows(chips[1 + way], core, d), pass_send.at[d], far_recv.at[d], (ahead, behind)[way])

    def from_far(d):
        return move(q_rows(chips[3], core, d), pass_send.at[d], far_recv.at[d], (ahead, behind)[d % 2])

    fetches = [
        pltpu.make_async_copy(src.at[:, columns(uly)], stage.at[i], keep_sem.at[i])
        for i, src in enumerate((nq_ref, nk_ref, nv_ref))
    ]
    keeps = [
        pltpu.make_async_copy(stage.at[i], dst, keep_sem.at[i])
        for i, dst in enumerate(
            (q_ref.at[q_rows(z, core, 0), :], k_ref.at[span_rows(uly), :], v_ref.at[span_rows(uly), :])
        )
    ]
    for fetch in fetches:
        fetch.start()
    for fetch in fetches:
        fetch.wait()
    pl.semaphore_wait(barrier, ulys - 1 + 3)

    def own_piece(send, recv, device):
        return pltpu.make_async_remote_copy(
            src_ref=stage.at[0], dst_ref=q_ref.at[q_rows(z, core, 0), :],
            send_sem=send, recv_sem=recv, device_id=device, device_id_type=MESH,
        )

    own_piece(own_send.at[0, 0], ring_recv.at[0, 0], ahead).start()
    own_piece(own_send.at[1, 0], ring_recv.at[1, 0], behind).start()
    for d in range(1, 1 + FLIGHT):
        q_copy(d).start()
    own_piece(sib_send.at[0, 0], sib_recv.at[0, 0], sibling).start()
    for keep in keeps:
        keep.start()

    for d in range(1, ulys):
        move(q_rows(z, core, d), q_send.at[d], q_recv.at[d], sibling).wait_recv()
        if d + FLIGHT < ulys:
            q_copy(d).wait_send()
            q_copy(d + FLIGHT).start()
        to_ring(0, d).start()
        to_ring(1, d).start()
        to_sibling(0, d).start()
    for which in range(2):
        for d in range(1, ulys):
            kv_copy(which, d).start()
    for d in range(ulys):
        for way in range(2):
            from_ring(way, d).wait_recv()
            if d % 2 == way:
                onward(way, d).start()
            to_sibling(1 + way, d).start()
    for d in range(ulys):
        from_far(d).wait_recv()
        to_sibling(3, d).start()

    for d in range(1, ulys):
        if d + FLIGHT >= ulys:
            q_copy(d).wait_send()
        for which in range(2):
            kv_copy(which, d).wait_send()
            kv_wait(which, d).wait_recv()
    for keep in keeps:
        keep.wait()
    for d in range(ulys):
        to_ring(0, d).wait_send()
        to_ring(1, d).wait_send()
        onward(d % 2, d).wait_send()
        for slot in range(4):
            to_sibling(slot, d).wait_send()
            from_sibling(slot, d).wait_recv()


def spread(new_queries, new_keys, new_values, zs, ulys):
    height = new_queries.shape[0]
    dma = pltpu.SemaphoreType.DMA
    anywhere = pl.BlockSpec(memory_space=pl.ANY)
    span = jax.ShapeDtypeStruct((height * ulys, WIDTH), jnp.bfloat16)
    return pl.pallas_call(
        functools.partial(spread_kernel, zs),
        out_shape=(jax.ShapeDtypeStruct((height * ulys * zs * 2, WIDTH), jnp.bfloat16), span, span),
        in_specs=[pl.BlockSpec(memory_space=pltpu.HBM)] * 3,
        out_specs=(anywhere,) * 3,
        scratch_shapes=[
            pltpu.VMEM((3, height, WIDTH), jnp.bfloat16),
            dma((3,)), dma((ulys,)), dma((ulys,)),
            dma((2, ulys)), dma((2, ulys)),
            dma((2, ulys)), dma((2, ulys)),
            dma((ulys,)), dma((ulys,)),
            dma((4, ulys)), dma((4, ulys)),
        ],
        compiler_params=pltpu.CompilerParams(
            collective_id=0, has_side_effects=True, vmem_limit_bytes=VMEM_LIMIT
        ),
        cost_estimate=pl.CostEstimate(flops=0, bytes_accessed=2 * 10**7, transcendentals=0),
    )(new_queries, new_keys, new_values)


def merge(pieces):
    logs = []
    for ref, at in pieces:
        both = ref[at, WIDTH:PIECE, :].astype(jnp.float32)
        logs.append(both[:8] + both[8:])
    best = functools.reduce(jnp.maximum, logs)
    weights = [jnp.exp2(log - best) for log in logs]
    total = functools.reduce(jnp.add, weights)
    inverse = 1.0 / total
    shares = [w * inverse for w in weights]
    return shares, best + jnp.log2(total)


def head_sum(pieces, shares, h):
    found = None
    for (ref, at), share in zip(pieces, shares):
        term = ref[at, h * DH : (h + 1) * DH, :].astype(jnp.float32) * share[h : h + 1, :]
        found = term if found is None else found + term
    return found


def join_kernel(
    zs, part_ref, out_ref, own, sib, far, near, send_far, send_near, done,
    own_sem, sib_send, sib_recv, far_send, far_recv, near_send, near_recv, out_send, out_recv, out_local,
):
    blk = lax.axis_index("blk")
    uly = lax.axis_index("uly")
    z, core = blk // 2, blk % 2
    ring = [lax.rem(z + d, zs) for d in (2, 1, zs - 1, 0)]
    sibling = {"blk": z * 2 + 1 - core}
    ahead = {"blk": ring[1] * 2 + core}
    behind = {"blk": ring[2] * 2 + core}
    ulys = lax.axis_size("uly")
    tiles = own.shape[1]

    barrier = pltpu.get_barrier_semaphore()
    for device in (sibling, ahead, behind):
        pl.semaphore_signal(barrier, inc=1, device_id=device, device_id_type=MESH)
    for d in range(1, ulys):
        pl.semaphore_signal(barrier, inc=1, device_id={"uly": lax.rem(uly + d, ulys)}, device_id_type=MESH)

    def turned(t):
        return lax.rem(t + uly, tiles)

    def own_copy(slot, t):
        index = (ring[slot] * 2 + core) * tiles + turned(t)
        return pltpu.make_async_copy(part_ref.at[index], own.at[slot, t], own_sem.at[slot, t])

    def sib_copy(slot, t):
        index = (ring[slot] * 2 + 1 - core) * tiles + turned(t)
        return pltpu.make_async_remote_copy(
            src_ref=part_ref.at[index], dst_ref=sib.at[slot, t],
            send_sem=sib_send.at[slot, t], recv_sem=sib_recv.at[slot, t],
            device_id=sibling, device_id_type=MESH,
        )

    def far_copy(t):
        return pltpu.make_async_remote_copy(
            src_ref=send_far.at[t], dst_ref=far.at[t],
            send_sem=far_send.at[t], recv_sem=far_recv.at[t],
            device_id=ahead if t < 2 else behind, device_id_type=MESH,
        )

    def near_copy(way, t):
        return pltpu.make_async_remote_copy(
            src_ref=send_near.at[way, t], dst_ref=near.at[way, t],
            send_sem=near_send.at[way, t], recv_sem=near_recv.at[way, t],
            device_id=ahead if way == 0 else behind, device_id_type=MESH,
        )

    order = [(0, 0), (0, 2), (0, 1), (0, 3)]
    order += [(slot, t) for t in (0, 2, 1, 3) for slot in (1, 2)]
    order += [(3, t) for t in (0, 2, 1, 3)]
    for slot, t in order:
        own_copy(slot, t).start()
    pl.semaphore_wait(barrier, 3 + ulys - 1)
    for slot, t in order:
        sib_copy(slot, t).start()

    def ready(slot, t):
        own_copy(slot, t).wait()
        sib_copy(slot, t).wait_recv()
        return [(own.at[slot], t), (sib.at[slot], t)]

    def store(pieces, dst):
        shares, log = merge(pieces)
        for h in range(HEADS):
            dst[h * DH : (h + 1) * DH, :] = head_sum(pieces, shares, h).astype(jnp.bfloat16)
        dst[WIDTH:PIECE, :] = split_low(log)

    for t in (0, 2, 1, 3):
        store(ready(0, t), send_far.at[t])
        far_copy(t).start()
    for t in (0, 2, 1, 3):
        passed = t // 2
        for way in (1 - passed, passed):
            pieces = ready(way + 1, t)
            if way == passed:
                far_copy(t).wait_recv()
                pieces = pieces + [(far, t)]
            place = (0, 2, 1, 3).index(t)
            store(pieces, send_near.at[way, t])
            if place >= DEPTH:
                near_copy(way, (0, 2, 1, 3)[place - DEPTH]).wait_send()
            near_copy(way, t).start()

    half = out_ref.shape[0]

    def out_copy(i, u):
        return pltpu.make_async_remote_copy(
            src_ref=done.at[i], dst_ref=out_ref.at[:, pl.ds(pl.multiple_of(uly * WIDTH, WIDTH), WIDTH)],
            send_sem=out_send.at[i], recv_sem=out_recv.at[uly],
            device_id={"uly": u}, device_id_type=MESH,
        )

    def out_keep(i):
        return pltpu.make_async_copy(
            done.at[i], out_ref.at[:, pl.ds(pl.multiple_of(uly * WIDTH, WIDTH), WIDTH)], out_local
        )

    for t in (0, 2, 1, 3):
        pieces = ready(3, t)
        near_copy(0, t).wait_recv()
        near_copy(1, t).wait_recv()
        pieces = pieces + [(near.at[0], t), (near.at[1], t)]
        shares, log = merge(pieces)
        for h in range(HEADS):
            flat = head_sum(pieces, shares, h).astype(jnp.bfloat16).T
            for j in range(2):
                done[2 * t + j, :, h * DH : (h + 1) * DH] = flat[j * half : (j + 1) * half]
        for j in range(2):
            u = 2 * turned(t) + j

            @pl.when(uly != u)
            def _():
                out_copy(2 * t + j, u).start()

            @pl.when(uly == u)
            def _():
                out_keep(2 * t + j).start()

    out_keep(0).wait()
    for i in range(ulys):
        u = 2 * turned(i // 2) + i % 2

        @pl.when(uly != u)
        def _():
            out_copy(i, u).wait_send()
            pltpu.make_async_remote_copy(
                src_ref=done.at[i], dst_ref=out_ref.at[:, pl.ds(pl.multiple_of(u * WIDTH, WIDTH), WIDTH)],
                send_sem=out_send.at[i], recv_sem=out_recv.at[u],
                device_id={"uly": u}, device_id_type=MESH,
            ).wait_recv()

    for slot, t in order:
        sib_copy(slot, t).wait_send()
    for t in range(tiles):
        far_copy(t).wait_send()
        if (0, 2, 1, 3).index(t) >= tiles - DEPTH:
            near_copy(0, t).wait_send()
            near_copy(1, t).wait_send()


def join(part, rows, zs, ulys):
    tiles = part.shape[0] // (2 * zs)
    piece = (PIECE, TILE)
    dma = pltpu.SemaphoreType.DMA
    return pl.pallas_call(
        functools.partial(join_kernel, zs),
        out_shape=jax.ShapeDtypeStruct((rows, ulys * WIDTH), jnp.bfloat16),
        in_specs=[pl.BlockSpec(memory_space=pl.ANY)],
        out_specs=pl.BlockSpec(memory_space=pl.ANY),
        scratch_shapes=[
            pltpu.VMEM((4, tiles) + piece, jnp.bfloat16),
            pltpu.VMEM((4, tiles) + piece, jnp.bfloat16),
            pltpu.VMEM((tiles,) + piece, jnp.bfloat16),
            pltpu.VMEM((2, tiles) + piece, jnp.bfloat16),
            pltpu.VMEM((tiles,) + piece, jnp.bfloat16),
            pltpu.VMEM((2, tiles) + piece, jnp.bfloat16),
            pltpu.VMEM((ulys, rows, WIDTH), jnp.bfloat16),
            dma((4, tiles)), dma((4, tiles)), dma((4, tiles)),
            dma((tiles,)), dma((tiles,)),
            dma((2, tiles)), dma((2, tiles)),
            dma((ulys,)), dma((ulys,)), dma,
        ],
        compiler_params=pltpu.CompilerParams(
            collective_id=1, has_side_effects=True, vmem_limit_bytes=48 * 1024 * 1024
        ),
        cost_estimate=pl.CostEstimate(flops=2 * 10**7, bytes_accessed=10**7, transcendentals=10**5),
    )(part)


def shards(new_queries, new_keys, new_values, context_keys, context_values, keep_flags):
    zs, ulys = lax.axis_size("blk") // 2, lax.axis_size("uly")
    queries, span_keys, span_values = spread(new_queries, new_keys, new_values, zs, ulys)
    blk = jnp.reshape(lax.axis_index("blk").astype(jnp.int32), (1,))
    part = attend(blk, keep_flags, queries, context_keys, span_keys, context_values, span_values)
    return join(part, new_queries.shape[0], zs, ulys)


def solution(mesh):
    in_specs = (
        P(("cfg", "blk", "uly"), None),
        P(("cfg", "blk", "uly"), None),
        P(("cfg", "blk", "uly"), None),
        P(("cfg", "blk"), "uly"),
        P(("cfg", "blk"), "uly"),
        P(),
    )
    out_specs = P(("cfg", "blk", "uly"), None)
    return jax.shard_map(shards, mesh=mesh, in_specs=in_specs, out_specs=out_specs, check_vma=False)
```
